32 devices in a mesh: segment: 2 (over x), seq: 4 (over y, core), mp: 4 (over z).
Axes of the slice: x: 2, y: 2, z: 4, core: 2. Of those that a mesh axis runs over, the one named last changes fastest.
Arguments:
- enc_states: bfloat16 [1024, 4096], P('seq', 'mp'), may hold values from -6 to 6
- dec_states: bfloat16 [1024, 4096], P('seq', 'mp'), may hold values from -21 to 21
- section_weights: bfloat16 [2, 4096, 2, 4096], P('segment', None, None, 'mp'), may hold values from -3 to 3
- group_lengths: int32 [8], P('seq'), may hold values from 1 to 128, 768 in all
Outputs:
- mixed: bfloat16 [1024, 4096], P('seq', ('segment', 'mp'))
The draws below stay inside these ranges and needn't reach their ends.
Inputs may be any that keep to these rules, and one draw needn't show every extreme that they name: Rows c * 128 to c * 128 + group_lengths[c] - 1 of the memory are real, the rest of block c is padding.
All inputs are finite; a program needn't handle non-finite values.
Results may differ from the reference program's by a relative error of at most 0.018.
Values may be sent and summed in bfloat16 or wider, within the bound.
No kernel may reach another device: no remote copies, remote signals or barrier semaphores. Data moves between devices by JAX's collectives and lax.ppermute only.
A program may use at most 128 MiB of HBM per device.

```python
import math
import jax
import jax.numpy as jnp
import numpy as np
from jax import lax

D = 4096
HEADS = 16
DH = 256
GROUP = 128
ENC_ROWS = 1024
DEC_ROWS = 1024
GROUPS = 8


def encoder_values(key):
    inner = jax.random.fold_in(key, 11)
    values = jnp.clip(jax.random.normal(inner, (ENC_ROWS, D), jnp.float32), -6.0, 6.0)
    return values


def draw_enc_states(key, part):
    return encoder_values(key).astype(jnp.bfloat16)


def draw_dec_states(key, part):
    inner = jax.random.fold_in(key, 23)
    values = jnp.clip(jax.random.normal(inner, (DEC_ROWS, D), jnp.float32), -6.0, 6.0)
    return values.astype(jnp.bfloat16)


def draw_section_weights(key, part):
    inner = jax.random.fold_in(key, 37)
    factor = D ** (-0.5)
    values = jnp.clip(jax.random.normal(inner, (2, D, 2, D), jnp.float32), -6.0, 6.0) * factor
    values = values.at[1, :, 0, :].multiply(3.0)
    return values.astype(jnp.bfloat16)


def profile(number_of, total, reach, lean):
    weights = [(1 << 20) // math.isqrt(grade ** lean) + 1 for grade in range(2, number_of + 1)]
    surplus, given = total - reach - (number_of - 1), [1] * (number_of - 1)
    while surplus > 0:
        free = [i for i in range(number_of - 1) if given[i] < reach]
        mass, budget = sum([weights[i] for i in free]), surplus
        for i in free:
            addition = min(reach - given[i], max(1, budget * weights[i] // mass), surplus)
            given[i] = given[i] + addition
            surplus = surplus - addition
    return np.array([reach] + given)


def uneven_parts(stream_key, amount, total, most, lean):
    if amount == 2:
        one = jax.random.randint(stream_key, (), max(1, total - most), min(most, total - 1) + 1)
        return jnp.stack([one, total - one])
    tallies = jnp.asarray(profile(amount, total, most, lean), jnp.int32)
    twos = (amount - 1) // 2
    donor, taker = tallies[1:1 + 2 * twos:2], tallies[2:2 + 2 * twos:2]
    slack = jnp.minimum(donor - 1, most - taker)
    shifted = jax.random.randint(jax.random.fold_in(stream_key, 1), (twos,), 0, 1 << 20) % (slack + 1)
    tallies = tallies.at[1:1 + 2 * twos:2].set(donor - shifted).at[2:2 + 2 * twos:2].set(taker + shifted)
    return tallies[jax.random.permutation(jax.random.fold_in(stream_key, 2), amount)]


def setup_inputs(seed: int = 0) -> dict:
    streams_of = jax.random.split(jax.random.key(seed), 5)
    enc_states = draw_enc_states(jax.random.fold_in(streams_of[4], 71), 0)
    dec_states = draw_dec_states(jax.random.fold_in(streams_of[4], 71), 0)
    section_weights = draw_section_weights(jax.random.fold_in(streams_of[4], 71), 0)
    group_lengths = uneven_parts(streams_of[3], GROUPS, GROUPS * GROUP * 3 // 4, GROUP, 0).astype(jnp.int32)
    return {"enc_states": enc_states, "dec_states": dec_states, "section_weights": section_weights, "group_lengths": group_lengths}


def split_heads(matrix, rows):
    return matrix.reshape(rows, HEADS, DH).transpose(1, 0, 2)


def reference(enc_states, dec_states, section_weights, group_lengths):
    key_weight = section_weights[0, :, 0, :]
    value_weight = section_weights[0, :, 1, :]
    query_weight = section_weights[1, :, 0, :]
    output_weight = section_weights[1, :, 1, :]
    memory_keys = jnp.dot(enc_states, key_weight, preferred_element_type=jnp.float32).astype(jnp.bfloat16)
    memory_values = jnp.dot(enc_states, value_weight, preferred_element_type=jnp.float32).astype(jnp.bfloat16)
    queries = jnp.dot(dec_states, query_weight, preferred_element_type=jnp.float32).astype(jnp.bfloat16)
    valid = (jnp.arange(GROUP)[None, :] < group_lengths[:, None]).reshape(ENC_ROWS)
    scale = DH ** -0.5

    def one_head(operands):
        query_head, key_head, value_head = operands
        scores = jnp.dot(query_head, key_head.T, preferred_element_type=jnp.float32) * scale
        scores = jnp.where(valid[None, :], scores, -1e30)
        highest = jnp.max(scores, axis=1, keepdims=True)
        weights = jnp.exp(scores - highest).astype(jnp.bfloat16)
        denominator = jnp.sum(weights.astype(jnp.float32), axis=1, keepdims=True)
        numerator = jnp.dot(weights, value_head, preferred_element_type=jnp.float32)
        return (numerator / denominator).astype(jnp.bfloat16)

    attended = lax.map(one_head, (split_heads(queries, DEC_ROWS), split_heads(memory_keys, ENC_ROWS), split_heads(memory_values, ENC_ROWS)))
    attended = attended.transpose(1, 0, 2).reshape(DEC_ROWS, D)
    projected = lax.dot_general(attended, output_weight, (((1,), (1,)), ((), ())), preferred_element_type=jnp.float32)
    mixed = dec_states.astype(jnp.float32) + projected
    return mixed.astype(jnp.bfloat16)
```

```python
import functools

import jax
import jax.numpy as jnp
from jax import lax
from jax.experimental import pallas as pl
from jax.experimental.pallas import tpu as pltpu
from jax.sharding import PartitionSpec as P

DH = 256
GROUP = 128
CHUNKS = 2
BF16 = jnp.bfloat16
F32 = jnp.float32

OUTER = [(0, 1), (1, 0), (2, 3), (3, 2)]
INNER = [(1, 2), (2, 1)]
OUTWARD = [(1, 0), (2, 3)]
INWARD = [(0, 1), (3, 2)]


def line_blocks(size, me):
    if size == 4:
        low = me < 2
        return [me, me ^ 1, jnp.where(low, 2, 1), jnp.where(low, 3, 0)]
    order = [me]
    for step in range(1, size // 2 + 1):
        order.append(lax.rem(me - step + size, size))
        if len(order) < size:
            order.append(lax.rem(me + step, size))
    return order


def line_gather(own, axis):
    size = lax.axis_size(axis)
    if size == 4:
        me = lax.axis_index(axis)
        inner = (me == 1) | (me == 2)
        partner = lax.ppermute(own, axis, OUTER)
        middle = lax.ppermute(own, axis, INNER)
        far = lax.ppermute(partner, axis, INNER)
        middle_out = lax.ppermute(middle, axis, OUTWARD)
        far_out = lax.ppermute(far, axis, OUTWARD)
        return [own, partner, jnp.where(inner, middle, middle_out), jnp.where(inner, far, far_out)]
    blocks = [own]
    up = down = own
    for step in range(1, size // 2 + 1):
        up = lax.ppermute(up, axis, [(i, (i + 1) % size) for i in range(size)])
        blocks.append(up)
        if len(blocks) < size:
            down = lax.ppermute(down, axis, [(i, (i - 1) % size) for i in range(size)])
            blocks.append(down)
    return blocks


def line_scatter(blocks, axis):
    size = lax.axis_size(axis)
    if size == 4:
        me = lax.axis_index(axis)
        low = me < 2
        inner = (me == 1) | (me == 2)

        def add(mine, got):
            return (mine.astype(F32) + got.astype(F32)).astype(BF16)

        def pick(a, b):
            return jnp.where(low, a, b)

        first = lax.ppermute(pick(blocks[3], blocks[0]), axis, INWARD)
        second = lax.ppermute(pick(blocks[2], blocks[1]), axis, INWARD)
        cross_far = lax.ppermute(add(pick(blocks[3], blocks[0]), first), axis, INNER)
        cross_near = lax.ppermute(add(pick(blocks[2], blocks[1]), second), axis, INNER)
        edge = pick(blocks[0], blocks[3])
        near = pick(blocks[1], blocks[2])
        last = lax.ppermute(jnp.where(inner, add(edge, cross_far), near), axis, OUTER)
        own = jnp.where(inner, near, edge).astype(F32)
        return own + last.astype(F32) + jnp.where(inner, cross_near, 0).astype(F32)
    return lax.psum_scatter(
        jnp.concatenate(blocks, axis=1), axis, scatter_dimension=1, tiled=True
    ).astype(F32)


def attention_kernel(heads, rows, lengths, queries, *refs):
    pieces, out = refs[:-1], refs[-1]
    half = heads * DH
    per_piece = rows // GROUP
    masks = []
    for index in range(len(pieces)):
        for group in range(per_piece):
            column = lax.broadcasted_iota(jnp.int32, (1, GROUP), 1)
            masks.append(column < lengths[index * per_piece + group])
    valid = jnp.concatenate(masks, axis=1)
    for head in range(heads):
        columns = slice(head * DH, head * DH + DH)
        value_columns = slice(half + head * DH, half + head * DH + DH)
        query = queries[:, columns]
        scores = jnp.concatenate(
            [
                lax.dot_general(
                    query, piece[:, columns], (((1,), (1,)), ((), ())), preferred_element_type=F32
                )
                for piece in pieces
            ],
            axis=1,
        )
        scores = jnp.where(valid, scores * DH ** (-0.5), -1e30)
        best = jnp.max(scores, axis=1, keepdims=True)
        weights = jnp.exp(scores - best).astype(BF16)
        total = jnp.sum(weights.astype(F32), axis=1, keepdims=True)
        accum = jnp.zeros((query.shape[0], DH), F32)
        for index, piece in enumerate(pieces):
            accum += jnp.dot(
                weights[:, index * rows : (index + 1) * rows],
                piece[:, value_columns],
                preferred_element_type=F32,
            )
        out[:, columns] = (accum / total).astype(BF16)


def attention(queries, pieces, lengths):
    rows = pieces[0].shape[0]
    heads = queries.shape[1] // DH
    keys = rows * len(pieces)
    vmem = pl.BlockSpec(memory_space=pltpu.VMEM)
    return pl.pallas_call(
        functools.partial(attention_kernel, heads, rows),
        out_shape=jax.ShapeDtypeStruct(queries.shape, BF16),
        in_specs=[pl.BlockSpec(memory_space=pltpu.SMEM)] + [vmem] * (1 + len(pieces)),
        out_specs=vmem,
        compiler_params=pltpu.CompilerParams(vmem_limit_bytes=40 * 1024 * 1024),
        cost_estimate=pl.CostEstimate(
            flops=4 * queries.shape[0] * keys * queries.shape[1],
            bytes_accessed=4 * queries.size + 4 * keys * queries.shape[1],
            transcendentals=queries.shape[0] * heads * keys,
        ),
        name="attention",
    )(lengths, queries, *pieces)


def exchange(first, second, seq):
    encoder_side = lax.axis_index("segment") == 0
    half = first.shape[1] // 2
    across = lax.ppermute(
        jnp.where(encoder_side, second, first), "segment", [(0, 1), (1, 0)]
    )
    here = jnp.where(encoder_side, first, across)
    queries = jnp.where(encoder_side, across[:, :half], second[:, :half])
    if seq == 4:
        along = lax.ppermute(first, ("segment", "seq"), [(q, q ^ 2) for q in range(4)])
        diagonal = lax.ppermute(second, ("segment", "seq"), [(q, 4 + (q ^ 2)) for q in range(4)])
        there = jnp.where(encoder_side, along, diagonal)
        swap = [(q, q ^ 1) for q in range(4)]
        return [here, there, lax.ppermute(here, "seq", swap), lax.ppermute(there, "seq", swap)], queries
    everything = lax.all_gather(here, "seq", axis=0)
    return [everything[place] for place in range(seq)], queries


def gather_lengths(lengths, seq):
    if seq == 4:
        there = lax.ppermute(lengths, "seq", [(q, q ^ 2) for q in range(4)])
        chip = jnp.concatenate([lengths, there])
        return jnp.concatenate([chip, lax.ppermute(chip, "seq", [(q, q ^ 1) for q in range(4)])])
    return lax.all_gather(lengths, "seq", axis=0, tiled=True)


def relayout_kernel(order, raw, out):
    columns = raw.shape[2]
    half = columns // 2
    apart = jnp.swapaxes(raw[...], 0, 1)
    out[:, :half] = apart[0, :, :half]
    out[:, half:columns] = apart[1, :, :half]
    out[:, columns : columns + half] = apart[0, :, half:]
    out[:, columns + half :] = apart[1, :, half:]


def relayout(weights, order):
    width, _, columns = weights.shape
    return pl.pallas_call(
        relayout_kernel,
        out_shape=jax.ShapeDtypeStruct((width, 2 * columns), BF16),
        grid_spec=pltpu.PrefetchScalarGridSpec(
            num_scalar_prefetch=1,
            grid=(width // columns,),
            in_specs=[pl.BlockSpec((columns, 2, columns), lambda i, order: (order[i], 0, 0))],
            out_specs=pl.BlockSpec((columns, 2 * columns), lambda i, order: (i, 0)),
        ),
        compiler_params=pltpu.CompilerParams(vmem_limit_bytes=48 * 1024 * 1024),
        cost_estimate=pl.CostEstimate(
            flops=0, bytes_accessed=8 * width * columns, transcendentals=0
        ),
        name="relayout",
    )(order, weights)


def local(enc_states, dec_states, section_weights, group_lengths):
    segment = lax.axis_index("segment")
    encoder_side = segment == 0
    place = lax.axis_index("mp")
    size = lax.axis_size("mp")
    seq = lax.axis_size("seq")
    width, _, columns = section_weights.shape[1:]
    rows = enc_states.shape[0]
    per_chunk = rows // CHUNKS
    half = columns // 2
    blocks_here = size // 2

    states = jnp.where(encoder_side, enc_states, dec_states)
    gathered = [
        line_gather(states[chunk * per_chunk : (chunk + 1) * per_chunk], "mp")
        for chunk in range(CHUNKS)
    ]
    lengths = gather_lengths(group_lengths, seq)

    order = jnp.stack([jnp.asarray(block, jnp.int32) for block in line_blocks(size, place)])
    weights = relayout(section_weights[0], order)
    inverse = jnp.argsort(order)

    def output_weights(block):
        rows_of = lax.dynamic_slice(
            weights, (inverse[block] * columns, 0), (columns, 2 * columns)
        )
        return rows_of[:, half:columns], rows_of[:, columns + half :]

    give = blocks_here // 2
    core = lax.rem(lax.axis_index("seq"), 2)
    sent = lax.ppermute(
        jnp.concatenate(
            [
                jnp.concatenate(output_weights(core * give + index), axis=1)
                for index in range(give)
            ],
            axis=0,
        ),
        "segment",
        [(1, 0)],
    )
    twin = lax.ppermute(sent, "seq", [(q, q ^ 1) for q in range(seq)])
    output_mine, output_other = [], []
    for index in range(blocks_here):
        source = (sent, twin) if index < give else (twin, sent)
        start = (index % give) * columns
        got = jnp.where(core == 0, source[0], source[1])[start : start + columns]
        first, second = output_weights(blocks_here + index)
        output_mine.append(jnp.where(encoder_side, got[:, :half], second))
        output_other.append(jnp.where(encoder_side, got[:, half:], first))

    projected = []
    for chunk in range(CHUNKS):
        total = None
        for index, block in enumerate(gathered[chunk]):
            term = jnp.dot(
                block,
                weights[index * columns : (index + 1) * columns],
                preferred_element_type=F32,
            )
            total = term if total is None else total + term
        projected.append(total.astype(BF16))

    pieces = [[] for _ in range(seq)]
    query_parts = []
    for chunk in range(CHUNKS):
        part = projected[chunk]
        memory, queries = exchange(part[:, :columns], part[:, columns:], seq)
        for source, piece in enumerate(memory):
            pieces[source].append(piece)
        query_parts.append(queries)
    flat = [piece for source in pieces for piece in source]

    residual = jnp.arange(blocks_here) == place - segment * blocks_here
    outputs = []
    for chunk in range(CHUNKS):
        attended = attention(query_parts[chunk], flat, lengths)
        swapped = lax.ppermute(attended, "segment", [(0, 1), (1, 0)])
        start = dec_states[chunk * per_chunk : (chunk + 1) * per_chunk].astype(F32)
        terms = []
        for index in range(blocks_here):
            term = lax.dot_general(
                attended, output_mine[index], (((1,), (1,)), ((), ())), preferred_element_type=F32
            )
            term += lax.dot_general(
                swapped, output_other[index], (((1,), (1,)), ((), ())), preferred_element_type=F32
            )
            term = (term + jnp.where(residual[index], start, 0)).astype(BF16)
            terms += [term[:, :half], term[:, half:]]
        outputs.append(line_scatter(terms, "mp"))
    return jnp.concatenate(outputs, axis=0).astype(BF16)


def solution(mesh):
    in_specs = (P("seq", "mp"), P("seq", "mp"), P("segment", None, None, "mp"), P("seq"))
    out_specs = P("seq", ("segment", "mp"))
    return jax.shard_map(local, mesh=mesh, in_specs=in_specs, out_specs=out_specs, check_vma=False)
```

```python
import functools
import math

import jax
import jax.numpy as jnp
from jax import lax
from jax.experimental import pallas as pl
from jax.experimental.pallas import tpu as pltpu
from jax.sharding import PartitionSpec as P

DH = 256
GROUP = 128
CHUNKS = 2
BF16 = jnp.bfloat16
F32 = jnp.float32


def tie(value, *after):
    return lax.optimization_barrier((value, *after))[0]


def swap(value, axis, distance):
    return lax.ppermute(value, axis, [(i, i ^ distance) for i in range(lax.axis_size(axis))])


def line_order(size, me):
    if size == 4:
        return [me, me ^ 1, me ^ 2, me ^ 3]
    order = [me]
    for step in range(1, size // 2 + 1):
        order.append(lax.rem(me - step + size, size))
        if len(order) < size:
            order.append(lax.rem(me + step, size))
    return order


def line_gather(own, axis, after=None):
    size = lax.axis_size(axis)
    if size == 4:
        across = swap(own if after is None else tie(own, *after), axis, 2)
        beside = swap(own, axis, 1)
        return [own, beside, across, swap(across, axis, 1)]
    blocks = [own]
    up = down = own
    for step in range(1, size // 2 + 1):
        up = lax.ppermute(up, axis, [(i, (i + 1) % size) for i in range(size)])
        blocks.append(up)
        if len(blocks) < size:
            down = lax.ppermute(down, axis, [(i, (i - 1) % size) for i in range(size)])
            blocks.append(down)
    return blocks


def line_scatter(blocks, axis):
    if lax.axis_size(axis) == 4:
        far = swap(blocks[3], axis, 1)
        beside = swap(tie(blocks[1], far), axis, 1)
        across = swap((blocks[2].astype(F32) + far.astype(F32)).astype(BF16), axis, 2)
        return blocks[0].astype(F32) + beside.astype(F32) + across.astype(F32)
    return lax.psum_scatter(
        jnp.concatenate(blocks, axis=1), axis, scatter_dimension=1, tiled=True
    ).astype(F32)


def attention_kernel(heads, rows, chunks, scalars, *refs):
    queries, pieces, outs = refs[: 2 * chunks], refs[2 * chunks : -chunks], refs[-chunks:]
    encoder_side = scalars[0] == 0
    half = heads * DH
    per_piece = rows // GROUP
    per_chunk = outs[0].shape[0]
    masks = []
    for index in range(len(pieces)):
        for group in range(per_piece):
            column = lax.broadcasted_iota(jnp.int32, (1, GROUP), 1)
            masks.append(column < scalars[1 + index * per_piece + group])
    valid = jnp.concatenate(masks, axis=1)
    for head in range(heads):
        columns = slice(head * DH, head * DH + DH)
        theirs = slice(2 * half + head * DH, 2 * half + head * DH + DH)
        value_columns = slice(half + head * DH, half + head * DH + DH)
        query = jnp.concatenate(
            [
                jnp.where(encoder_side, across[:, columns], part[:, theirs])
                for across, part in zip(queries[::2], queries[1::2])
            ],
            axis=0,
        )
        scores = jnp.concatenate(
            [
                lax.dot_general(
                    query, piece[:, columns], (((1,), (1,)), ((), ())), preferred_element_type=F32
                )
                for piece in pieces
            ],
            axis=1,
        )
        scores = jnp.where(valid, scores * DH ** (-0.5), -1e30)
        best = jnp.max(scores, axis=1, keepdims=True)
        weights = jnp.exp(scores - best).astype(BF16)
        total = jnp.sum(weights.astype(F32), axis=1, keepdims=True)
        accum = jnp.zeros((query.shape[0], DH), F32)
        for index, piece in enumerate(pieces):
            accum += jnp.dot(
                weights[:, index * rows : (index + 1) * rows],
                piece[:, value_columns],
                preferred_element_type=F32,
            )
        attended = (accum / total).astype(BF16)
        for chunk, out in enumerate(outs):
            out[:, columns] = attended[chunk * per_chunk : (chunk + 1) * per_chunk]


def attention(segment, queries, pieces, lengths):
    rows, columns = queries[0][0].shape
    chunks = len(queries)
    heads = columns // 2 // DH
    keys = pieces[0].shape[0] * len(pieces)
    vmem = pl.BlockSpec(memory_space=pltpu.VMEM)
    scalars = jnp.concatenate([jnp.asarray(segment, jnp.int32).reshape(1), lengths])
    return pl.pallas_call(
        functools.partial(attention_kernel, heads, pieces[0].shape[0], chunks),
        out_shape=[jax.ShapeDtypeStruct((rows, columns // 2), BF16)] * chunks,
        in_specs=[pl.BlockSpec(memory_space=pltpu.SMEM)] + [vmem] * (2 * chunks + len(pieces)),
        out_specs=[vmem] * chunks,
        compiler_params=pltpu.CompilerParams(vmem_limit_bytes=16 * 1024 * 1024),
        cost_estimate=pl.CostEstimate(
            flops=2 * chunks * rows * keys * columns,
            bytes_accessed=4 * chunks * rows * columns + 2 * keys * columns,
            transcendentals=chunks * rows * heads * keys,
        ),
        name="attention",
    )(scalars, *[array for pair in queries for array in pair], *pieces)


def exchange(first, second, seq):
    encoder_side = lax.axis_index("segment") == 0
    across = swap(jnp.where(encoder_side, second, first), "segment", 1)
    here = jnp.where(encoder_side, first, across)
    if seq == 4:
        there = swap(here, "seq", 2)
        return [here, there, swap(here, "seq", 1), swap(there, "seq", 1)], across
    everything = lax.all_gather(here, "seq", axis=0)
    return [everything[place] for place in range(seq)], across


def gather_lengths(lengths, seq):
    if seq == 4:
        chip = jnp.concatenate([lengths, swap(lengths, "seq", 2)])
        return jnp.concatenate([chip, swap(chip, "seq", 1)])
    return lax.all_gather(lengths, "seq", axis=0, tiled=True)


def pick_kernel(which, first, second, *refs):
    outs, sems = refs[:-1], refs[-1]
    rows = outs[0].shape[0]
    for index, ref in enumerate((first, second)):

        @pl.when(which[0] == index)
        def _(ref=ref):
            for chunk, out in enumerate(outs):
                pltpu.make_async_copy(
                    ref.at[pl.ds(chunk * rows, rows)], out, sems.at[chunk]
                ).start()

    for chunk, out in enumerate(outs):
        pltpu.make_async_copy(out, out, sems.at[chunk]).wait()


def pick(which, first, second):
    rows, columns = first.shape
    return pl.pallas_call(
        pick_kernel,
        out_shape=[pltpu.VMEM((rows // CHUNKS, columns), BF16)] * CHUNKS,
        in_specs=[pl.BlockSpec(memory_space=pltpu.SMEM)]
        + [pl.BlockSpec(memory_space=pl.ANY)] * 2,
        out_specs=[pl.BlockSpec(memory_space=pltpu.VMEM)] * CHUNKS,
        scratch_shapes=[pltpu.SemaphoreType.DMA((CHUNKS,))],
        name="pick",
    )(jnp.asarray(which, jnp.int32).reshape(1), first, second)


def relayout_kernel(order, raw, out, second):
    columns = raw.shape[2]
    half = columns // 2
    rows = pl.ds(pl.multiple_of(pl.program_id(0) * columns, columns), columns)
    apart = jnp.swapaxes(raw[...], 0, 1)
    out[rows, :half] = apart[0, :, :half]
    out[rows, half:columns] = apart[1, :, :half]
    out[rows, columns : columns + half] = apart[0, :, half:]
    out[rows, columns + half :] = apart[1, :, half:]
    second[...] = apart[1]


def relayout(weights, order, first, count):
    _, _, columns = weights.shape
    return pl.pallas_call(
        relayout_kernel,
        out_shape=[
            pltpu.VMEM((count * columns, 2 * columns), BF16),
            jax.ShapeDtypeStruct((count * columns, columns), BF16),
        ],
        grid_spec=pltpu.PrefetchScalarGridSpec(
            num_scalar_prefetch=1,
            grid=(count,),
            in_specs=[
                pl.BlockSpec((columns, 2, columns), lambda i, order: (order[first + i], 0, 0))
            ],
            out_specs=[
                pl.BlockSpec(memory_space=pltpu.VMEM),
                pl.BlockSpec((columns, columns), lambda i, order: (i, 0)),
            ],
        ),
        compiler_params=pltpu.CompilerParams(vmem_limit_bytes=36 * 1024 * 1024),
        cost_estimate=pl.CostEstimate(
            flops=0, bytes_accessed=10 * count * columns * columns, transcendentals=0
        ),
        name="relayout",
    )(order, weights)


def output_rows_kernel(block, raw, *outs):
    rows = outs[0].shape[0]
    for index, out in enumerate(outs):
        out[...] = jnp.swapaxes(raw[index * rows : (index + 1) * rows], 0, 1)[1]


def output_rows(weights, block, rows, pieces):
    _, _, columns = weights.shape
    return pl.pallas_call(
        output_rows_kernel,
        out_shape=[jax.ShapeDtypeStruct((rows // pieces, columns), BF16)] * pieces,
        grid_spec=pltpu.PrefetchScalarGridSpec(
            num_scalar_prefetch=1,
            grid=(1,),
            in_specs=[pl.BlockSpec((rows, 2, columns), lambda i, block: (block[0], 0, 0))],
            out_specs=[pl.BlockSpec((rows // pieces, columns), lambda i, block: (0, 0))] * pieces,
        ),
        compiler_params=pltpu.CompilerParams(vmem_limit_bytes=56 * 1024 * 1024),
        cost_estimate=pl.CostEstimate(
            flops=0, bytes_accessed=6 * rows * columns, transcendentals=0
        ),
        name="output_rows",
    )(jnp.asarray(block, jnp.int32).reshape(1), weights)


def output_kernel(each, scalars, mine, other, weights, states, *outs):
    half = mine.shape[1]
    encoder_side = scalars[0] == 0
    first = jnp.where(encoder_side, mine[...], other[...])
    second = jnp.where(encoder_side, other[...], mine[...])
    attended = jnp.concatenate([first, second], axis=1)
    for index, out in enumerate(outs):
        rows = slice(index * each, (index + 1) * each)
        term = lax.dot_general(
            attended, weights[rows, :], (((1,), (1,)), ((), ())), preferred_element_type=F32
        )
        start = pl.multiple_of(scalars[1 + 2 * index], 128)
        residual = states[:, pl.ds(start, each)].astype(F32)
        out[...] = (term + jnp.where(scalars[2 + 2 * index] == 1, residual, 0)).astype(BF16)


def output_blocks(mine, other, weights, states, chunk, scalars, count):
    rows, half = mine.shape
    each = weights.shape[0] // count
    vmem = pl.BlockSpec(memory_space=pltpu.VMEM)
    here = pl.BlockSpec((rows, states.shape[1]), lambda i: (chunk, 0))
    return pl.pallas_call(
        functools.partial(output_kernel, each),
        out_shape=[jax.ShapeDtypeStruct((rows, each), BF16)] * count,
        grid=(1,),
        in_specs=[pl.BlockSpec(memory_space=pltpu.SMEM)] + [vmem] * 3 + [here],
        out_specs=[vmem] * count,
        compiler_params=pltpu.CompilerParams(vmem_limit_bytes=16 * 1024 * 1024),
        cost_estimate=pl.CostEstimate(
            flops=4 * rows * half * weights.shape[0],
            bytes_accessed=2 * weights.size + 4 * rows * weights.shape[0],
            transcendentals=0,
        ),
        name="output_blocks",
    )(scalars, mine, other, weights, states)


def assemble_kernel(each, count, scalars, *refs):
    sources, out, sems = refs[:-2], refs[-2], refs[-1]
    parts = [out.at[pl.ds(k * each, each)] for k in range(count)]
    for k in range(count):
        source, row = scalars[2 * k], pl.multiple_of(scalars[1 + 2 * k], each)
        for index, ref in enumerate(sources):

            @pl.when(source == index)
            def _(ref=ref, k=k, row=row):
                pltpu.make_async_copy(ref.at[pl.ds(row, each)], parts[k], sems.at[k]).start()

    for k in range(count):
        pltpu.make_async_copy(parts[k], parts[k], sems.at[k]).wait()


def assemble(sources, scalars, each, count):
    columns = sources[0].shape[1]
    return pl.pallas_call(
        functools.partial(assemble_kernel, each, count),
        out_shape=pltpu.VMEM((each * count, columns), BF16),
        in_specs=[pl.BlockSpec(memory_space=pltpu.SMEM)]
        + [pl.BlockSpec(memory_space=pl.ANY)] * len(sources),
        out_specs=pl.BlockSpec(memory_space=pltpu.VMEM),
        scratch_shapes=[pltpu.SemaphoreType.DMA((count,))],
        compiler_params=pltpu.CompilerParams(vmem_limit_bytes=16 * 1024 * 1024),
        cost_estimate=pl.CostEstimate(
            flops=0, bytes_accessed=4 * each * count * columns, transcendentals=0
        ),
        name="assemble",
    )(scalars, *sources)


def local(enc_states, dec_states, section_weights, group_lengths):
    segment = lax.axis_index("segment")
    encoder_side = segment == 0
    place = lax.axis_index("mp")
    size = lax.axis_size("mp")
    seq = lax.axis_size("seq")
    raw = section_weights[0]
    width, _, columns = raw.shape
    each = width // (2 * size)

    order = jnp.stack([jnp.asarray(block, jnp.int32) for block in line_order(size, place)])
    parts = 4 if seq == 4 else 1
    me = lax.axis_index("seq")
    states = pick(segment, enc_states, dec_states)
    gathered = [line_gather(states[0], "mp")]
    own_weights, own_output = relayout(raw, order, 0, 1)
    ahead = output_rows(raw, me if parts == 4 else 0, width // (2 * parts), parts // 2 or 1)
    gathered.append(line_gather(states[1], "mp", (gathered[0][2], own_output, *ahead)))
    ahead = [lax.ppermute(part, "segment", [(1, 0)]) for part in ahead]
    along = [swap(part, "seq", 2) for part in ahead] if parts == 4 else []
    weights, output = relayout(tie(raw, gathered[0][2]), order, 1, size - 1)
    pieces_of = [own_weights] + [
        weights[index * columns : (index + 1) * columns] for index in range(size - 1)
    ]
    lengths = gather_lengths(group_lengths, seq)

    projected = []
    for chunk in range(CHUNKS):
        blocks = list(gathered[chunk])
        if size == 4:
            after = (gathered[0][3], gathered[1][2], *along[:1])
            blocks[1:3] = tie(tuple(blocks[1:3]), *after)
        total = None
        for block, weight in zip(blocks, pieces_of):
            term = jnp.dot(block, weight, preferred_element_type=F32)
            total = term if total is None else total + term
        projected.append(total.astype(BF16))

    pieces = [[] for _ in range(seq)]
    query_parts = []
    for chunk in range(CHUNKS):
        part = projected[chunk]
        if chunk:
            part = tie(part, across, *along[1:])
        memory, across = exchange(part[:, :columns], part[:, columns:], seq)
        for source, piece in enumerate(memory):
            pieces[source].append(piece)
        query_parts.append((across, part))
    flat = [piece for source in pieces for piece in source]

    low = ahead + along
    if parts == 4:
        low = [tie(part, flat[-1]) for part in low]
        low += [swap(part, "seq", 1) for part in low]
    targets = [place ^ k if size == 4 else jnp.int32(k) for k in range(size)]
    inverse = None if size == 4 else jnp.argsort(order)
    grain = math.gcd(each, ahead[0].shape[0])
    sources, residual = [], [segment]
    for target in targets:
        for offset in range(0, each, grain):
            start = target * each + offset
            block = (width // 2 + start) // columns
            block = block ^ place if inverse is None else inverse[block]
            row = jnp.maximum(block - 1, 0) * columns + lax.rem(start, columns)
            part, low_row = 0, start
            if parts == 4:
                per = width // (2 * parts)
                part = (start // per) ^ me
                part = ((part & 1) << 1) | (part >> 1)
                part = part * len(ahead) + lax.rem(start, per) // ahead[0].shape[0]
                low_row = lax.rem(start, ahead[0].shape[0])
            sources.append(jnp.where(encoder_side, part, len(low) + jnp.minimum(block, 1)))
            sources.append(jnp.where(encoder_side, low_row, row))
        start = segment * (width // 2) + target * each - place * columns
        inside = (start >= 0) & (start < columns)
        residual += [jnp.where(inside, start, 0), inside]
    sources = jnp.stack([jnp.asarray(value, jnp.int32) for value in sources])
    residual = jnp.stack([jnp.asarray(value, jnp.int32) for value in residual])
    final = assemble(low + [own_output, output], sources, grain, width // (2 * grain))

    outputs = []
    for chunk, attended in enumerate(attention(segment, query_parts, flat, lengths)):
        blocks = output_blocks(
            attended, swap(attended, "segment", 1), final, dec_states, chunk, residual, size
        )
        outputs.append(line_scatter(blocks, "mp"))
    return jnp.concatenate(outputs, axis=0).astype(BF16)


def solution(mesh):
    in_specs = (P("seq", "mp"), P("seq", "mp"), P("segment", None, None, "mp"), P("seq"))
    out_specs = P("seq", ("segment", "mp"))
    return jax.shard_map(local, mesh=mesh, in_specs=in_specs, out_specs=out_specs, check_vma=False)
```

```python
import functools
import math

import jax
import jax.numpy as jnp
from jax import lax
from jax.experimental import pallas as pl
from jax.experimental.pallas import tpu as pltpu
from jax.sharding import PartitionSpec as P

DH = 256
GROUP = 128
CHUNKS = 2
BF16 = jnp.bfloat16
F32 = jnp.float32


def tie(value, *after):
    return lax.optimization_barrier((value, *after))[0]


def swap(value, axis, distance):
    return lax.ppermute(value, axis, [(i, i ^ distance) for i in range(lax.axis_size(axis))])


def line_order(size, me):
    if size == 4:
        return [me, me ^ 1, me ^ 2, me ^ 3]
    order = [me]
    for step in range(1, size // 2 + 1):
        order.append(lax.rem(me - step + size, size))
        if len(order) < size:
            order.append(lax.rem(me + step, size))
    return order


def line_gather(own, axis):
    size = lax.axis_size(axis)
    blocks = [own]
    up = down = own
    for step in range(1, size // 2 + 1):
        up = lax.ppermute(up, axis, [(i, (i + 1) % size) for i in range(size)])
        blocks.append(up)
        if len(blocks) < size:
            down = lax.ppermute(down, axis, [(i, (i - 1) % size) for i in range(size)])
            blocks.append(down)
    return blocks


def line_scatter(blocks, axis):
    if lax.axis_size(axis) == 4:
        far = swap(blocks[3], axis, 1)
        beside = swap(tie(blocks[1], far), axis, 1)
        across = swap((blocks[2].astype(F32) + far.astype(F32)).astype(BF16), axis, 2)
        return blocks[0].astype(F32) + beside.astype(F32) + across.astype(F32)
    return lax.psum_scatter(
        jnp.concatenate(blocks, axis=1), axis, scatter_dimension=1, tiled=True
    ).astype(F32)


def attention_kernel(heads, rows, chunks, scalars, *refs):
    queries, pieces, outs = refs[: 2 * chunks], refs[2 * chunks : -chunks], refs[-chunks:]
    encoder_side = scalars[0] == 0
    half = heads * DH
    per_piece = rows // GROUP
    per_chunk = outs[0].shape[0]
    masks = []
    for index in range(len(pieces)):
        for group in range(per_piece):
            column = lax.broadcasted_iota(jnp.int32, (1, GROUP), 1)
            masks.append(column < scalars[1 + index * per_piece + group])
    valid = jnp.concatenate(masks, axis=1)
    for head in range(heads):
        columns = slice(head * DH, head * DH + DH)
        theirs = slice(2 * half + head * DH, 2 * half + head * DH + DH)
        value_columns = slice(half + head * DH, half + head * DH + DH)
        query = jnp.concatenate(
            [
                jnp.where(encoder_side, across[:, columns], part[:, theirs])
                for across, part in zip(queries[::2], queries[1::2])
            ],
            axis=0,
        )
        scores = jnp.concatenate(
            [
                lax.dot_general(
                    query, piece[:, columns], (((1,), (1,)), ((), ())), preferred_element_type=F32
                )
                for piece in pieces
            ],
            axis=1,
        )
        scores = jnp.where(valid, scores * DH ** (-0.5), -1e30)
        best = jnp.max(scores, axis=1, keepdims=True)
        weights = jnp.exp(scores - best).astype(BF16)
        total = jnp.sum(weights.astype(F32), axis=1, keepdims=True)
        accum = jnp.zeros((query.shape[0], DH), F32)
        for index, piece in enumerate(pieces):
            accum += jnp.dot(
                weights[:, index * rows : (index + 1) * rows],
                piece[:, value_columns],
                preferred_element_type=F32,
            )
        attended = (accum / total).astype(BF16)
        for chunk, out in enumerate(outs):
            out[:, columns] = attended[chunk * per_chunk : (chunk + 1) * per_chunk]


def attention(segment, queries, pieces, lengths):
    rows, columns = queries[0][0].shape
    chunks = len(queries)
    heads = columns // 2 // DH
    keys = pieces[0].shape[0] * len(pieces)
    vmem = pl.BlockSpec(memory_space=pltpu.VMEM)
    scalars = jnp.concatenate([jnp.asarray(segment, jnp.int32).reshape(1), lengths])
    return pl.pallas_call(
        functools.partial(attention_kernel, heads, pieces[0].shape[0], chunks),
        out_shape=[jax.ShapeDtypeStruct((rows, columns // 2), BF16)] * chunks,
        in_specs=[pl.BlockSpec(memory_space=pltpu.SMEM)] + [vmem] * (2 * chunks + len(pieces)),
        out_specs=[vmem] * chunks,
        compiler_params=pltpu.CompilerParams(vmem_limit_bytes=16 * 1024 * 1024),
        cost_estimate=pl.CostEstimate(
            flops=2 * chunks * rows * keys * columns,
            bytes_accessed=4 * chunks * rows * columns + 2 * keys * columns,
            transcendentals=chunks * rows * heads * keys,
        ),
        name="attention",
    )(scalars, *[array for pair in queries for array in pair], *pieces)


def exchange(part, payload, seq):
    encoder_side = lax.axis_index("segment") == 0
    across = swap(payload, "segment", 1)
    here = jnp.where(encoder_side, part[:, : payload.shape[1]], across)
    if seq == 4:
        there = swap(here, "seq", 2)
        return [here, there, swap(here, "seq", 1), swap(there, "seq", 1)], across
    everything = lax.all_gather(here, "seq", axis=0)
    return [everything[place] for place in range(seq)], across


def gather_lengths(lengths, seq):
    if seq == 4:
        chip = jnp.concatenate([lengths, swap(lengths, "seq", 2)])
        return jnp.concatenate([chip, swap(chip, "seq", 1)])
    return lax.all_gather(lengths, "seq", axis=0, tiled=True)


def pick_kernel(scalars, raw, first, second, *refs):
    outs, row_out, buffer, sems = refs[:-3], refs[-3], refs[-2], refs[-1]
    rows = outs[0].shape[0]
    piece = row_out.shape[0]
    start = pl.multiple_of(scalars[1] * piece, piece)
    fetch = pltpu.make_async_copy(raw.at[pl.ds(start, piece)], buffer, sems.at[len(outs)])
    for index, ref in enumerate((first, second)):

        @pl.when(scalars[0] == index)
        def _(ref=ref):
            for chunk, out in enumerate(outs):
                pltpu.make_async_copy(
                    ref.at[pl.ds(chunk * rows, rows)], out, sems.at[chunk]
                ).start()

    fetch.start()
    fetch.wait()
    row_out[...] = jnp.swapaxes(buffer[...], 0, 1)[1]
    for chunk, out in enumerate(outs):
        pltpu.make_async_copy(out, out, sems.at[chunk]).wait()


def pick(which, first, second, weights, block, piece):
    rows, columns = first.shape
    width = weights.shape[2]
    hbm = pl.BlockSpec(memory_space=pltpu.HBM)
    scalars = jnp.stack([jnp.asarray(which, jnp.int32), jnp.asarray(block, jnp.int32)])
    return pl.pallas_call(
        pick_kernel,
        out_shape=[pltpu.VMEM((rows // CHUNKS, columns), BF16)] * CHUNKS
        + [pltpu.VMEM((piece, width), BF16)],
        in_specs=[pl.BlockSpec(memory_space=pltpu.SMEM)] + [hbm] * 3,
        out_specs=[pl.BlockSpec(memory_space=pltpu.VMEM)] * (CHUNKS + 1),
        scratch_shapes=[
            pltpu.VMEM((piece, 2, width), BF16),
            pltpu.SemaphoreType.DMA((CHUNKS + 1,)),
        ],
        compiler_params=pltpu.CompilerParams(vmem_limit_bytes=62_300_000),
        cost_estimate=pl.CostEstimate(flops=0, bytes_accessed=rows * columns, transcendentals=0),
        name="pick",
    )(scalars, weights, first, second)


def relayout_kernel(half_blocks, order, raw, *refs):
    out, second, buffers, staged, sems = refs[-5:]
    columns = raw.shape[2]
    half = columns // 2
    rows = buffers.shape[1]
    per = columns // rows
    steps = out.shape[0] // rows

    def copy(step):
        start = pl.multiple_of(order[step // per] * columns + step % per * rows, rows)
        return pltpu.make_async_copy(
            raw.at[pl.ds(start, rows)], buffers.at[step % 2], sems.at[step % 2]
        )

    def store(step):
        return pltpu.make_async_copy(
            staged.at[step % 2], second.at[pl.ds(step * rows, rows)], sems.at[2 + step % 2]
        )

    def when(step):
        return pl.when(order[step // per] >= half_blocks)

    copy(0).start()
    for step in range(steps):
        if step + 1 < steps:
            copy(step + 1).start()
        copy(step).wait()
        there = slice(step * rows, (step + 1) * rows)
        apart = jnp.swapaxes(buffers[step % 2], 0, 1)
        out[there, :half] = apart[0, :, :half]
        out[there, half:columns] = apart[1, :, :half]
        out[there, columns : columns + half] = apart[0, :, half:]
        out[there, columns + half :] = apart[1, :, half:]
        if step > 1:
            when(step - 2)(lambda: store(step - 2).wait())

        @when(step)
        def _(step=step, apart=apart):
            staged[step % 2] = apart[1]
            store(step).start()

    for step in range(max(0, steps - 2), steps):
        when(step)(lambda: store(step).wait())


def relayout(weights, order, *after):
    width, _, columns = weights.shape
    rows = min(columns, 512)
    hbm = pl.BlockSpec(memory_space=pltpu.HBM)
    return pl.pallas_call(
        functools.partial(relayout_kernel, width // columns // 2),
        out_shape=[
            pltpu.VMEM((width, 2 * columns), BF16),
            jax.ShapeDtypeStruct((width, columns), BF16),
        ],
        in_specs=[pl.BlockSpec(memory_space=pltpu.SMEM), hbm]
        + [pl.BlockSpec(memory_space=pl.ANY)] * len(after),
        out_specs=[pl.BlockSpec(memory_space=pltpu.VMEM), hbm],
        scratch_shapes=[
            pltpu.VMEM((2, rows, 2, columns), BF16),
            pltpu.VMEM((2, rows, columns), BF16),
            pltpu.SemaphoreType.DMA((4,)),
        ],
        compiler_params=pltpu.CompilerParams(vmem_limit_bytes=32 * 1024 * 1024),
        cost_estimate=pl.CostEstimate(
            flops=0, bytes_accessed=8 * width * columns, transcendentals=0
        ),
        name="relayout",
    )(order, weights, *after)


def project_kernel(chunks, *refs):
    blocks, weights, outs, held = refs[: -2 - chunks], refs[-2 - chunks], refs[-1 - chunks : -1], refs[-1]
    rows, width = outs[0].shape
    count = len(blocks) // chunks
    depth = blocks[0].shape[1]
    for index, block in enumerate(blocks):
        chunk = index % chunks
        held[index // chunks, chunk * rows : (chunk + 1) * rows] = block[...]
    tile = 512
    for start in range(0, width, tile):
        there = slice(start, start + tile)
        total = None
        for index in range(count):
            weight = weights[index * depth : (index + 1) * depth, there]
            term = jnp.dot(held[index], weight, preferred_element_type=F32)
            total = term if total is None else total + term
        for chunk, out in enumerate(outs):
            out[:, there] = total[chunk * rows : (chunk + 1) * rows]


def project(gathered, weights):
    chunks, count = len(gathered[0]), len(gathered)
    rows, depth = gathered[0][0].shape
    width = weights.shape[1]
    vmem = pl.BlockSpec(memory_space=pltpu.VMEM)
    return pl.pallas_call(
        functools.partial(project_kernel, chunks),
        out_shape=[jax.ShapeDtypeStruct((rows, width), F32)] * chunks,
        in_specs=[vmem] * (chunks * count + 1),
        out_specs=[vmem] * chunks,
        scratch_shapes=[pltpu.VMEM((count, chunks * rows, depth), BF16)],
        compiler_params=pltpu.CompilerParams(vmem_limit_bytes=20 * 1024 * 1024),
        cost_estimate=pl.CostEstimate(
            flops=2 * chunks * count * rows * depth * width,
            bytes_accessed=2 * count * depth * width,
            transcendentals=0,
        ),
        name="project",
    )(*[block for blocks in gathered for block in blocks], weights)


def project_last_kernel(which, total, block, weights, out, payload):
    depth = block.shape[1]
    half = out.shape[1] // 2
    tile = 512
    weight_rows = slice(weights.shape[0] - depth, weights.shape[0])
    for start in range(0, half, tile):
        there = slice(start, start + tile)
        behind = slice(half + start, half + start + tile)
        first, second = (
            (
                total[:, part]
                + jnp.dot(block[...], weights[weight_rows, part], preferred_element_type=F32)
            ).astype(BF16)
            for part in (there, behind)
        )
        out[:, there] = first
        out[:, behind] = second
        payload[:, there] = jnp.where(which[0] == 0, second, first)


def project_last(segment, total, block, weights):
    rows, width = total.shape
    vmem = pl.BlockSpec(memory_space=pltpu.VMEM)
    return pl.pallas_call(
        project_last_kernel,
        out_shape=[
            jax.ShapeDtypeStruct((rows, width), BF16),
            jax.ShapeDtypeStruct((rows, width // 2), BF16),
        ],
        in_specs=[pl.BlockSpec(memory_space=pltpu.SMEM)] + [vmem] * 3,
        out_specs=[vmem] * 2,
        compiler_params=pltpu.CompilerParams(vmem_limit_bytes=16 * 1024 * 1024),
        cost_estimate=pl.CostEstimate(
            flops=2 * rows * block.shape[1] * width,
            bytes_accessed=2 * block.shape[1] * width,
            transcendentals=0,
        ),
        name="project_last",
    )(jnp.asarray(segment, jnp.int32).reshape(1), total, block, weights)


def output_rows_kernel(block, raw, first, out, buffer, sem):
    rows = out.shape[0]
    start = pl.multiple_of(block[0] * rows, rows)
    copy = pltpu.make_async_copy(raw.at[pl.ds(start, rows)], buffer, sem)
    copy.start()
    copy.wait()
    out[...] = jnp.swapaxes(buffer[...], 0, 1)[1]


def output_rows(weights, block, rows, after):
    _, _, columns = weights.shape
    return pl.pallas_call(
        output_rows_kernel,
        out_shape=pltpu.VMEM((rows, columns), BF16),
        in_specs=[
            pl.BlockSpec(memory_space=pltpu.SMEM),
            pl.BlockSpec(memory_space=pltpu.HBM),
            pl.BlockSpec(memory_space=pl.ANY),
        ],
        out_specs=pl.BlockSpec(memory_space=pltpu.VMEM),
        scratch_shapes=[pltpu.VMEM((rows, 2, columns), BF16), pltpu.SemaphoreType.DMA],
        compiler_params=pltpu.CompilerParams(vmem_limit_bytes=50 * 1024 * 1024),
        cost_estimate=pl.CostEstimate(
            flops=0, bytes_accessed=rows * columns, transcendentals=0
        ),
        name="output_rows",
    )(jnp.asarray(block, jnp.int32).reshape(1), weights, after)


def output_kernel(each, scalars, mine, other, weights, states, *outs):
    half = mine.shape[1]
    encoder_side = scalars[0] == 0
    first = jnp.where(encoder_side, mine[...], other[...])
    second = jnp.where(encoder_side, other[...], mine[...])
    attended = jnp.concatenate([first, second], axis=1)
    for index, out in enumerate(outs):
        rows = slice(index * each, (index + 1) * each)
        term = lax.dot_general(
            attended, weights[rows, :], (((1,), (1,)), ((), ())), preferred_element_type=F32
        )
        start = pl.multiple_of(scalars[1 + 2 * index], 128)
        residual = states[:, pl.ds(start, each)].astype(F32)
        out[...] = (term + jnp.where(scalars[2 + 2 * index] == 1, residual, 0)).astype(BF16)


def output_blocks(mine, other, weights, states, chunk, scalars, count):
    rows, half = mine.shape
    each = weights.shape[0] // count
    vmem = pl.BlockSpec(memory_space=pltpu.VMEM)
    here = pl.BlockSpec((rows, states.shape[1]), lambda i: (chunk, 0))
    return pl.pallas_call(
        functools.partial(output_kernel, each),
        out_shape=[jax.ShapeDtypeStruct((rows, each), BF16)] * count,
        grid=(1,),
        in_specs=[pl.BlockSpec(memory_space=pltpu.SMEM)] + [vmem] * 3 + [here],
        out_specs=[vmem] * count,
        compiler_params=pltpu.CompilerParams(vmem_limit_bytes=16 * 1024 * 1024),
        cost_estimate=pl.CostEstimate(
            flops=4 * rows * half * weights.shape[0],
            bytes_accessed=2 * weights.size + 4 * rows * weights.shape[0],
            transcendentals=0,
        ),
        name="output_blocks",
    )(scalars, mine, other, weights, states)


def assemble_kernel(each, count, scalars, *refs):
    sources, out, sems = refs[:-2], refs[-2], refs[-1]
    parts = [out.at[pl.ds(k * each, each)] for k in range(count)]
    for k in range(count):
        source, row = scalars[2 * k], pl.multiple_of(scalars[1 + 2 * k], each)
        for index, ref in enumerate(sources):

            @pl.when(source == index)
            def _(ref=ref, k=k, row=row):
                pltpu.make_async_copy(ref.at[pl.ds(row, each)], parts[k], sems.at[k]).start()

    for k in range(count):
        pltpu.make_async_copy(parts[k], parts[k], sems.at[k]).wait()


def assemble(sources, scalars, each, count):
    columns = sources[0].shape[1]
    return pl.pallas_call(
        functools.partial(assemble_kernel, each, count),
        out_shape=pltpu.VMEM((each * count, columns), BF16),
        in_specs=[pl.BlockSpec(memory_space=pltpu.SMEM)]
        + [pl.BlockSpec(memory_space=pl.ANY)] * len(sources),
        out_specs=pl.BlockSpec(memory_space=pltpu.VMEM),
        scratch_shapes=[pltpu.SemaphoreType.DMA((count,))],
        compiler_params=pltpu.CompilerParams(vmem_limit_bytes=48 * 1024 * 1024),
        cost_estimate=pl.CostEstimate(
            flops=0, bytes_accessed=4 * each * count * columns, transcendentals=0
        ),
        name="assemble",
    )(scalars, *sources)


def local(enc_states, dec_states, section_weights, group_lengths):
    segment = lax.axis_index("segment")
    encoder_side = segment == 0
    place = lax.axis_index("mp")
    size = lax.axis_size("mp")
    seq = lax.axis_size("seq")
    raw = section_weights[0]
    width, _, columns = raw.shape
    each = width // (2 * size)

    order = jnp.stack([jnp.asarray(block, jnp.int32) for block in line_order(size, place)])
    parts = 4 if seq == 4 else 1
    me = lax.axis_index("seq")
    lengths = gather_lengths(group_lengths, seq)
    pieces_ahead = 2
    ahead_rows = width // (2 * parts * pieces_ahead)
    first = me * pieces_ahead if parts == 4 else 0
    *states, ahead = pick(segment, enc_states, dec_states, raw, first, ahead_rows)
    rows = states[0].shape[0]
    ahead = [ahead, output_rows(raw, first + 1, ahead_rows, ahead)]
    along = []
    if size == 4:
        beside = [swap(part, "mp", 1) for part in states]
        across = [swap(states[0], "mp", 2)]
        last = [swap(across[0], "mp", 1)]
        for part in states[1:]:
            part = tie(part, across[-1], beside[0], *ahead)
            across.append(swap(part, "mp", 2))
            last.append(swap(across[-1], "mp", 1))
        blocks = [states, beside, across]
    else:
        blocks = line_gather(jnp.concatenate(states, axis=0), "mp")
        blocks = [
            [block[chunk * rows : (chunk + 1) * rows] for chunk in range(CHUNKS)]
            for block in blocks
        ]
        across, last = blocks[1], blocks.pop()
    ahead = [lax.ppermute(part, "segment", [(1, 0)]) for part in ahead]
    if parts == 4:
        along = [
            swap(tie(part, across[chunk % CHUNKS], lengths), "seq", 2)
            for chunk, part in enumerate(ahead)
        ]
    weights, output = relayout(raw, jnp.concatenate([order, lengths]), across[0])

    if size == 4:
        blocks = [tie(states, last[0], *along[:1])] + blocks[1:]
    totals = project(blocks, weights)
    pieces = [[] for _ in range(seq)]
    query_parts = []
    for chunk in range(CHUNKS):
        part, payload = project_last(segment, totals[chunk], last[chunk], weights)
        if chunk:
            payload = tie(payload, got, *along[1:])
        memory, got = exchange(part, payload, seq)
        for source, piece in enumerate(memory):
            pieces[source].append(piece)
        query_parts.append((got, part))
    flat = [piece for source in pieces for piece in source]

    low = ahead + along
    if parts == 4:
        low = [tie(part, pieces[1][0]) for part in low]
        low += [swap(part, "seq", 1) for part in low]
    targets = [place ^ k if size == 4 else jnp.int32(k) for k in range(size)]
    inverse = None if size == 4 else jnp.argsort(order)
    grain = math.gcd(each, ahead_rows)
    sources, residual = [], [segment]
    for target in targets:
        for offset in range(0, each, grain):
            start = target * each + offset
            block = (width // 2 + start) // columns
            block = block ^ place if inverse is None else inverse[block]
            row = block * columns + lax.rem(start, columns)
            part = 0
            per = width // (2 * parts)
            if parts == 4:
                part = (start // per) ^ me
                part = ((part & 1) << 1) | (part >> 1)
            part = part * pieces_ahead + lax.rem(start, per) // ahead_rows
            low_row = lax.rem(start, ahead_rows)
            sources.append(jnp.where(encoder_side, part, len(low)))
            sources.append(jnp.where(encoder_side, low_row, row))
        start = segment * (width // 2) + target * each - place * columns
        inside = (start >= 0) & (start < columns)
        residual += [jnp.where(inside, start, 0), inside]
    sources = jnp.stack([jnp.asarray(value, jnp.int32) for value in sources])
    residual = jnp.stack([jnp.asarray(value, jnp.int32) for value in residual])
    final = assemble(low + [output], sources, grain, width // (2 * grain))

    outputs = []
    for chunk, attended in enumerate(attention(segment, query_parts, flat, lengths)):
        blocks = output_blocks(
            attended, swap(attended, "segment", 1), final, dec_states, chunk, residual, size
        )
        outputs.append(line_scatter(blocks, "mp"))
    return jnp.concatenate(outputs, axis=0).astype(BF16)


def solution(mesh):
    in_specs = (P("seq", "mp"), P("seq", "mp"), P("segment", None, None, "mp"), P("seq"))
    out_specs = P("seq", ("segment", "mp"))
    return jax.shard_map(local, mesh=mesh, in_specs=in_specs, out_specs=out_specs, check_vma=False)
```

```python
import functools
import math

import jax
import jax.numpy as jnp
from jax import lax
from jax.experimental import pallas as pl
from jax.experimental.pallas import tpu as pltpu
from jax.sharding import PartitionSpec as P

DH = 256
GROUP = 128
CHUNKS = 2
BF16 = jnp.bfloat16
F32 = jnp.float32


def tie(value, *after):
    return lax.optimization_barrier((value, *after))[0]


def swap(value, axis, distance):
    return lax.ppermute(value, axis, [(i, i ^ distance) for i in range(lax.axis_size(axis))])


def line_order(size, me):
    if size == 4:
        return [me, me ^ 1, me ^ 2, me ^ 3]
    order = [me]
    for step in range(1, size // 2 + 1):
        order.append(lax.rem(me - step + size, size))
        if len(order) < size:
            order.append(lax.rem(me + step, size))
    return order


def line_gather(own, axis):
    size = lax.axis_size(axis)
    blocks = [own]
    up = down = own
    for step in range(1, size // 2 + 1):
        up = lax.ppermute(up, axis, [(i, (i + 1) % size) for i in range(size)])
        blocks.append(up)
        if len(blocks) < size:
            down = lax.ppermute(down, axis, [(i, (i - 1) % size) for i in range(size)])
            blocks.append(down)
    return blocks


def line_scatter(blocks, axis):
    if lax.axis_size(axis) == 4:
        far = swap(blocks[3], axis, 1)
        beside = swap(tie(blocks[1], far), axis, 1)
        across = swap((blocks[2].astype(F32) + far.astype(F32)).astype(BF16), axis, 2)
        return blocks[0].astype(F32) + beside.astype(F32) + across.astype(F32)
    return lax.psum_scatter(
        jnp.concatenate(blocks, axis=1), axis, scatter_dimension=1, tiled=True
    ).astype(F32)


def attention_kernel(heads, rows, chunks, scalars, *refs):
    queries, pieces, outs = refs[: 2 * chunks], refs[2 * chunks : -chunks], refs[-chunks:]
    encoder_side = scalars[0] == 0
    half = heads * DH
    per_piece = rows // GROUP
    per_chunk = outs[0].shape[0]
    masks = []
    for index in range(len(pieces)):
        for group in range(per_piece):
            column = lax.broadcasted_iota(jnp.int32, (1, GROUP), 1)
            masks.append(column < scalars[1 + index * per_piece + group])
    valid = jnp.concatenate(masks, axis=1)
    for head in range(heads):
        columns = slice(head * DH, head * DH + DH)
        theirs = slice(2 * half + head * DH, 2 * half + head * DH + DH)
        value_columns = slice(half + head * DH, half + head * DH + DH)
        query = jnp.concatenate(
            [
                jnp.where(encoder_side, across[:, columns], part[:, theirs])
                for across, part in zip(queries[::2], queries[1::2])
            ],
            axis=0,
        )
        scores = jnp.concatenate(
            [
                lax.dot_general(
                    query, piece[:, columns], (((1,), (1,)), ((), ())), preferred_element_type=F32
                )
                for piece in pieces
            ],
            axis=1,
        )
        scores = jnp.where(valid, scores * DH ** (-0.5), -1e30)
        best = jnp.max(scores, axis=1, keepdims=True)
        weights = jnp.exp(scores - best).astype(BF16)
        total = jnp.sum(weights.astype(F32), axis=1, keepdims=True)
        accum = jnp.zeros((query.shape[0], DH), F32)
        for index, piece in enumerate(pieces):
            accum += jnp.dot(
                weights[:, index * rows : (index + 1) * rows],
                piece[:, value_columns],
                preferred_element_type=F32,
            )
        attended = (accum / total).astype(BF16)
        for chunk, out in enumerate(outs):
            out[:, columns] = attended[chunk * per_chunk : (chunk + 1) * per_chunk]


def attention(segment, queries, pieces, lengths):
    rows, columns = queries[0][0].shape
    chunks = len(queries)
    heads = columns // 2 // DH
    keys = pieces[0].shape[0] * len(pieces)
    vmem = pl.BlockSpec(memory_space=pltpu.VMEM)
    scalars = jnp.concatenate([jnp.asarray(segment, jnp.int32).reshape(1), lengths])
    return pl.pallas_call(
        functools.partial(attention_kernel, heads, pieces[0].shape[0], chunks),
        out_shape=[jax.ShapeDtypeStruct((rows, columns // 2), BF16)] * chunks,
        in_specs=[pl.BlockSpec(memory_space=pltpu.SMEM)] + [vmem] * (2 * chunks + len(pieces)),
        out_specs=[vmem] * chunks,
        compiler_params=pltpu.CompilerParams(vmem_limit_bytes=16 * 1024 * 1024),
        cost_estimate=pl.CostEstimate(
            flops=2 * chunks * rows * keys * columns,
            bytes_accessed=4 * chunks * rows * columns + 2 * keys * columns,
            transcendentals=chunks * rows * heads * keys,
        ),
        name="attention",
    )(scalars, *[array for pair in queries for array in pair], *pieces)


def exchange(part, payload, seq, *after):
    encoder_side = lax.axis_index("segment") == 0
    across = swap(payload, "segment", 1)
    here = jnp.where(encoder_side, part[:, : payload.shape[1]], across)
    if seq == 4:
        there = swap(tie(here, *after) if after else here, "seq", 2)
        return [here, there, swap(here, "seq", 1), swap(there, "seq", 1)], across
    everything = lax.all_gather(here, "seq", axis=0)
    return [everything[place] for place in range(seq)], across


def gather_lengths(lengths, seq):
    if seq == 4:
        chip = jnp.concatenate([lengths, swap(lengths, "seq", 2)])
        return jnp.concatenate([chip, swap(chip, "seq", 1)])
    return lax.all_gather(lengths, "seq", axis=0, tiled=True)


def pick_kernel(scalars, raw, first, second, *refs):
    outs, row_out, buffer, sems = refs[:-3], refs[-3], refs[-2], refs[-1]
    rows = outs[0].shape[0]
    piece = row_out.shape[0]
    start = pl.multiple_of(scalars[1] * piece, piece)
    fetch = pltpu.make_async_copy(raw.at[pl.ds(start, piece)], buffer, sems.at[len(outs)])
    for index, ref in enumerate((first, second)):

        @pl.when(scalars[0] == index)
        def _(ref=ref):
            for chunk, out in enumerate(outs):
                pltpu.make_async_copy(
                    ref.at[pl.ds(chunk * rows, rows)], out, sems.at[chunk]
                ).start()

    fetch.start()
    fetch.wait()
    row_out[...] = jnp.swapaxes(buffer[...], 0, 1)[1]
    for chunk, out in enumerate(outs):
        pltpu.make_async_copy(out, out, sems.at[chunk]).wait()


def pick(which, first, second, weights, block, piece):
    rows, columns = first.shape
    width = weights.shape[2]
    hbm = pl.BlockSpec(memory_space=pltpu.HBM)
    scalars = jnp.stack([jnp.asarray(which, jnp.int32), jnp.asarray(block, jnp.int32)])
    return pl.pallas_call(
        pick_kernel,
        out_shape=[pltpu.VMEM((rows // CHUNKS, columns), BF16)] * CHUNKS
        + [pltpu.VMEM((piece, width), BF16)],
        in_specs=[pl.BlockSpec(memory_space=pltpu.SMEM)] + [hbm] * 3,
        out_specs=[pl.BlockSpec(memory_space=pltpu.VMEM)] * (CHUNKS + 1),
        scratch_shapes=[
            pltpu.VMEM((piece, 2, width), BF16),
            pltpu.SemaphoreType.DMA((CHUNKS + 1,)),
        ],
        compiler_params=pltpu.CompilerParams(vmem_limit_bytes=62_300_000),
        cost_estimate=pl.CostEstimate(flops=0, bytes_accessed=rows * columns, transcendentals=0),
        name="pick",
    )(scalars, weights, first, second)


def relayout_kernel(half_blocks, order, raw, *refs):
    out, second, buffers, staged, sems = refs[-5:]
    columns = raw.shape[2]
    half = columns // 2
    ahead, rows = buffers.shape[:2]
    per = columns // rows
    steps = out.shape[0] // rows

    def copy(step):
        start = pl.multiple_of(order[step // per] * columns + step % per * rows, rows)
        slot = step % ahead
        return pltpu.make_async_copy(
            raw.at[pl.ds(start, rows)], buffers.at[slot], sems.at[slot]
        )

    def store(step):
        return pltpu.make_async_copy(
            staged.at[step % 2], second.at[pl.ds(step * rows, rows)], sems.at[ahead + step % 2]
        )

    def when(step):
        return pl.when(order[step // per] >= half_blocks)

    for step in range(min(ahead - 1, steps)):
        copy(step).start()
    for step in range(steps):
        if step + ahead - 1 < steps:
            copy(step + ahead - 1).start()
        copy(step).wait()
        there = slice(step * rows, (step + 1) * rows)
        apart = jnp.swapaxes(buffers[step % ahead], 0, 1)
        out[there, :half] = apart[0, :, :half]
        out[there, half:columns] = apart[1, :, :half]
        out[there, columns : columns + half] = apart[0, :, half:]
        out[there, columns + half :] = apart[1, :, half:]
        if step > 1:
            when(step - 2)(lambda: store(step - 2).wait())

        @when(step)
        def _(step=step, apart=apart):
            staged[step % 2] = apart[1]
            store(step).start()

    for step in range(max(0, steps - 2), steps):
        when(step)(lambda: store(step).wait())


def relayout(weights, order, *after):
    width, _, columns = weights.shape
    rows = min(columns, 512)
    hbm = pl.BlockSpec(memory_space=pltpu.HBM)
    return pl.pallas_call(
        functools.partial(relayout_kernel, width // columns // 2),
        out_shape=[
            pltpu.VMEM((width, 2 * columns), BF16),
            jax.ShapeDtypeStruct((width, columns), BF16),
        ],
        in_specs=[pl.BlockSpec(memory_space=pltpu.SMEM), hbm]
        + [pl.BlockSpec(memory_space=pl.ANY)] * len(after),
        out_specs=[pl.BlockSpec(memory_space=pltpu.VMEM), hbm],
        scratch_shapes=[
            pltpu.VMEM((4, rows, 2, columns), BF16),
            pltpu.VMEM((2, rows, columns), BF16),
            pltpu.SemaphoreType.DMA((6,)),
        ],
        compiler_params=pltpu.CompilerParams(vmem_limit_bytes=32 * 1024 * 1024),
        cost_estimate=pl.CostEstimate(
            flops=0, bytes_accessed=8 * width * columns, transcendentals=0
        ),
        name="relayout",
    )(order, weights, *after)


def project_kernel(first, count, started, final, which, *refs):
    refs = refs[:-1]
    blocks, weights, refs = refs[:count], refs[count], refs[count + 1 :]
    depth = blocks[0].shape[1]
    half = weights.shape[1] // 2
    tile = min(half, 512)

    def columns(start):
        total = refs[0][:, start : start + tile] if started else None
        for index, block in enumerate(blocks):
            row = (first + index) * depth
            term = jnp.dot(
                block[...],
                weights[row : row + depth, start : start + tile],
                preferred_element_type=F32,
            )
            total = term if total is None else total + term
        return total

    for start in range(0, half, tile):
        there = slice(start, start + tile)
        behind = slice(half + start, half + start + tile)
        lower, upper = columns(start), columns(half + start)
        if final:
            out, payload = refs[-2:]
            lower, upper = lower.astype(BF16), upper.astype(BF16)
            payload[:, there] = jnp.where(which[0] == 0, upper, lower)
        else:
            out = refs[-1]
        out[:, there] = lower
        out[:, behind] = upper


def project(segment, blocks, first, weights, total, final):
    rows, depth = blocks[0].shape
    width = weights.shape[1]
    started = total is not None
    vmem = pl.BlockSpec(memory_space=pltpu.VMEM)
    if final:
        shapes = [
            jax.ShapeDtypeStruct((rows, width), BF16),
            jax.ShapeDtypeStruct((rows, width // 2), BF16),
        ]
    else:
        shapes = [jax.ShapeDtypeStruct((rows, width), F32)]
    *outs, weights = pl.pallas_call(
        functools.partial(project_kernel, first, len(blocks), started, final),
        out_shape=shapes + [pltpu.VMEM(weights.shape, BF16)],
        in_specs=[pl.BlockSpec(memory_space=pltpu.SMEM)] + [vmem] * (len(blocks) + 1 + started),
        out_specs=[vmem] * (len(shapes) + 1),
        input_output_aliases={1 + len(blocks): len(shapes)},
        compiler_params=pltpu.CompilerParams(vmem_limit_bytes=16 * 1024 * 1024),
        cost_estimate=pl.CostEstimate(
            flops=2 * len(blocks) * rows * depth * width,
            bytes_accessed=2 * len(blocks) * depth * width,
            transcendentals=0,
        ),
        name="project",
    )(
        jnp.asarray(segment, jnp.int32).reshape(1),
        *blocks,
        weights,
        *([total] if started else []),
    )
    return weights, *outs


def output_rows_kernel(block, raw, *refs):
    out, buffer, sem = refs[-3:]
    rows = out.shape[0]
    start = pl.multiple_of(block[0] * rows, rows)
    copy = pltpu.make_async_copy(raw.at[pl.ds(start, rows)], buffer, sem)
    copy.start()
    copy.wait()
    out[...] = jnp.swapaxes(buffer[...], 0, 1)[1]


def output_rows(weights, block, rows, *after):
    _, _, columns = weights.shape
    return pl.pallas_call(
        output_rows_kernel,
        out_shape=pltpu.VMEM((rows, columns), BF16),
        in_specs=[
            pl.BlockSpec(memory_space=pltpu.SMEM),
            pl.BlockSpec(memory_space=pltpu.HBM),
        ]
        + [pl.BlockSpec(memory_space=pl.ANY)] * len(after),
        out_specs=pl.BlockSpec(memory_space=pltpu.VMEM),
        scratch_shapes=[pltpu.VMEM((rows, 2, columns), BF16), pltpu.SemaphoreType.DMA],
        compiler_params=pltpu.CompilerParams(vmem_limit_bytes=50 * 1024 * 1024),
        cost_estimate=pl.CostEstimate(
            flops=0, bytes_accessed=rows * columns, transcendentals=0
        ),
        name="output_rows",
    )(jnp.asarray(block, jnp.int32).reshape(1), weights, *after)


def output_kernel(each, scalars, mine, other, weights, states, *outs):
    half = mine.shape[1]
    encoder_side = scalars[0] == 0
    first = jnp.where(encoder_side, mine[...], other[...])
    second = jnp.where(encoder_side, other[...], mine[...])
    attended = jnp.concatenate([first, second], axis=1)
    for index, out in enumerate(outs):
        rows = slice(index * each, (index + 1) * each)
        term = lax.dot_general(
            attended, weights[rows, :], (((1,), (1,)), ((), ())), preferred_element_type=F32
        )
        start = pl.multiple_of(scalars[1 + 2 * index], 128)
        residual = states[:, pl.ds(start, each)].astype(F32)
        out[...] = (term + jnp.where(scalars[2 + 2 * index] == 1, residual, 0)).astype(BF16)


def output_blocks(mine, other, weights, states, chunk, scalars, count):
    rows, half = mine.shape
    each = weights.shape[0] // count
    vmem = pl.BlockSpec(memory_space=pltpu.VMEM)
    here = pl.BlockSpec((rows, states.shape[1]), lambda i: (chunk, 0))
    return pl.pallas_call(
        functools.partial(output_kernel, each),
        out_shape=[jax.ShapeDtypeStruct((rows, each), BF16)] * count,
        grid=(1,),
        in_specs=[pl.BlockSpec(memory_space=pltpu.SMEM)] + [vmem] * 3 + [here],
        out_specs=[vmem] * count,
        compiler_params=pltpu.CompilerParams(vmem_limit_bytes=16 * 1024 * 1024),
        cost_estimate=pl.CostEstimate(
            flops=4 * rows * half * weights.shape[0],
            bytes_accessed=2 * weights.size + 4 * rows * weights.shape[0],
            transcendentals=0,
        ),
        name="output_blocks",
    )(scalars, mine, other, weights, states)


def assemble_kernel(each, count, scalars, *refs):
    sources, out, sems = refs[:-2], refs[-2], refs[-1]
    parts = [out.at[pl.ds(k * each, each)] for k in range(count)]
    for k in range(count):
        source, row = scalars[2 * k], pl.multiple_of(scalars[1 + 2 * k], each)
        for index, ref in enumerate(sources):

            @pl.when(source == index)
            def _(ref=ref, k=k, row=row):
                pltpu.make_async_copy(ref.at[pl.ds(row, each)], parts[k], sems.at[k]).start()

    for k in range(count):
        pltpu.make_async_copy(parts[k], parts[k], sems.at[k]).wait()


def assemble(sources, scalars, each, count):
    columns = sources[0].shape[1]
    return pl.pallas_call(
        functools.partial(assemble_kernel, each, count),
        out_shape=pltpu.VMEM((each * count, columns), BF16),
        in_specs=[pl.BlockSpec(memory_space=pltpu.SMEM)]
        + [pl.BlockSpec(memory_space=pl.ANY)] * len(sources),
        out_specs=pl.BlockSpec(memory_space=pltpu.VMEM),
        scratch_shapes=[pltpu.SemaphoreType.DMA((count,))],
        compiler_params=pltpu.CompilerParams(vmem_limit_bytes=48 * 1024 * 1024),
        cost_estimate=pl.CostEstimate(
            flops=0, bytes_accessed=4 * each * count * columns, transcendentals=0
        ),
        name="assemble",
    )(scalars, *sources)


def local(enc_states, dec_states, section_weights, group_lengths):
    segment = lax.axis_index("segment")
    encoder_side = segment == 0
    place = lax.axis_index("mp")
    size = lax.axis_size("mp")
    seq = lax.axis_size("seq")
    raw = section_weights[0]
    width, _, columns = raw.shape
    each = width // (2 * size)

    order = jnp.stack([jnp.asarray(block, jnp.int32) for block in line_order(size, place)])
    parts = 4 if seq == 4 else 1
    me = lax.axis_index("seq")
    lengths = gather_lengths(group_lengths, seq)
    pieces_ahead = 2
    ahead_rows = width // (2 * parts * pieces_ahead)
    first = me * pieces_ahead if parts == 4 else 0
    *states, ahead = pick(segment, enc_states, dec_states, raw, first, ahead_rows)
    rows = states[0].shape[0]
    ahead = [ahead, output_rows(raw, first + 1, ahead_rows, ahead, lengths)]
    along = []
    if size == 4:
        beside = [swap(part, "mp", 1) for part in states]
        across = [swap(states[0], "mp", 2)]
        last = [swap(across[0], "mp", 1)]
        for part in states[1:]:
            part = tie(part, across[-1], beside[0], *ahead)
            across.append(swap(part, "mp", 2))
            last.append(swap(across[-1], "mp", 1))
        blocks = [states, beside, across]
    else:
        blocks = line_gather(jnp.concatenate(states, axis=0), "mp")
        blocks = [
            [block[chunk * rows : (chunk + 1) * rows] for chunk in range(CHUNKS)]
            for block in blocks
        ]
        across, last = blocks[1], blocks.pop()
    ahead = [lax.ppermute(part, "segment", [(1, 0)]) for part in ahead]
    weights, output = relayout(raw, order, across[0])
    if parts == 4:
        along = [
            swap(tie(part, *after), "seq", 2)
            for part, after in zip(ahead, ((across[0],), (across[-1], output)))
        ]

    pieces = [[] for _ in range(seq)]
    query_parts = []
    for chunk in range(CHUNKS):
        terms = [block[chunk] for block in blocks]
        if chunk:
            weights, total = project(segment, terms, 0, weights, None, False)
            weights, part, payload = project(
                segment, [last[chunk]], size - 1, weights, total, True
            )
            payload = tie(payload, got)
        else:
            terms[0] = tie(terms[0], *along[:1])
            weights, part, payload = project(
                segment, terms + [last[chunk]], 0, weights, None, True
            )
        memory, got = exchange(part, payload, seq, *along[1:])
        for source, piece in enumerate(memory):
            pieces[source].append(piece)
        query_parts.append((got, part))
    flat = [piece for source in pieces for piece in source]

    low = ahead + along
    if parts == 4:
        low = [tie(part, pieces[1][0]) for part in low]
        low += [swap(part, "seq", 1) for part in low]
    targets = [place ^ k if size == 4 else jnp.int32(k) for k in range(size)]
    inverse = None if size == 4 else jnp.argsort(order)
    grain = math.gcd(each, ahead_rows)
    sources, residual = [], [segment]
    for target in targets:
        for offset in range(0, each, grain):
            start = target * each + offset
            block = (width // 2 + start) // columns
            block = block ^ place if inverse is None else inverse[block]
            row = block * columns + lax.rem(start, columns)
            part = 0
            per = width // (2 * parts)
            if parts == 4:
                part = (start // per) ^ me
                part = ((part & 1) << 1) | (part >> 1)
            part = part * pieces_ahead + lax.rem(start, per) // ahead_rows
            low_row = lax.rem(start, ahead_rows)
            sources.append(jnp.where(encoder_side, part, len(low)))
            sources.append(jnp.where(encoder_side, low_row, row))
        start = segment * (width // 2) + target * each - place * columns
        inside = (start >= 0) & (start < columns)
        residual += [jnp.where(inside, start, 0), inside]
    sources = jnp.stack([jnp.asarray(value, jnp.int32) for value in sources])
    residual = jnp.stack([jnp.asarray(value, jnp.int32) for value in residual])
    final = assemble(low + [output], sources, grain, width // (2 * grain))

    outputs = []
    for chunk, attended in enumerate(attention(segment, query_parts, flat, lengths)):
        blocks = output_blocks(
            attended, swap(attended, "segment", 1), final, dec_states, chunk, residual, size
        )
        outputs.append(line_scatter(blocks, "mp"))
    return jnp.concatenate(outputs, axis=0).astype(BF16)


def solution(mesh):
    in_specs = (P("seq", "mp"), P("seq", "mp"), P("segment", None, None, "mp"), P("seq"))
    out_specs = P("seq", ("segment", "mp"))
    return jax.shard_map(local, mesh=mesh, in_specs=in_specs, out_specs=out_specs, check_vma=False)
```

```python
import functools
import math

import jax
import jax.numpy as jnp
from jax import lax
from jax.experimental import pallas as pl
from jax.experimental.pallas import tpu as pltpu
from jax.sharding import PartitionSpec as P

DH = 256
GROUP = 128
CHUNKS = 2
BF16 = jnp.bfloat16
F32 = jnp.float32


def tie(value, *after):
    return lax.optimization_barrier((value, *after))[0]


def swap(value, axis, distance):
    return lax.ppermute(value, axis, [(i, i ^ distance) for i in range(lax.axis_size(axis))])


def line_order(size, me):
    if size == 4:
        return [me, me ^ 1, me ^ 2, me ^ 3]
    order = [me]
    for step in range(1, size // 2 + 1):
        order.append(lax.rem(me - step + size, size))
        if len(order) < size:
            order.append(lax.rem(me + step, size))
    return order


def line_gather(own, axis):
    size = lax.axis_size(axis)
    blocks = [own]
    up = down = own
    for step in range(1, size // 2 + 1):
        up = lax.ppermute(up, axis, [(i, (i + 1) % size) for i in range(size)])
        blocks.append(up)
        if len(blocks) < size:
            down = lax.ppermute(down, axis, [(i, (i - 1) % size) for i in range(size)])
            blocks.append(down)
    return blocks


def line_scatter(near, far, axis):
    if lax.axis_size(axis) == 4:
        across = [
            swap((blocks[2].astype(F32) + got.astype(F32)).astype(BF16), axis, 2)
            for blocks, got in zip(near, far)
        ]
        beside = [swap(tie(blocks[1], *far), axis, 1) for blocks in near]
        return [
            blocks[0].astype(F32) + one.astype(F32) + two.astype(F32)
            for blocks, one, two in zip(near, beside, across)
        ]
    return [
        lax.psum_scatter(
            jnp.concatenate([*blocks, last], axis=1), axis, scatter_dimension=1, tiled=True
        ).astype(F32)
        for blocks, last in zip(near, far)
    ]


def attention_kernel(heads, rows, chunks, scalars, *refs):
    queries, pieces, outs = refs[: 2 * chunks], refs[2 * chunks : -chunks], refs[-chunks:]
    encoder_side = scalars[0] == 0
    half = heads * DH
    per_piece = rows // GROUP
    per_chunk = outs[0].shape[0]
    masks = []
    for index in range(len(pieces)):
        for group in range(per_piece):
            column = lax.broadcasted_iota(jnp.int32, (1, GROUP), 1)
            masks.append(column < scalars[1 + index * per_piece + group])
    valid = jnp.concatenate(masks, axis=1)
    for head in range(heads):
        columns = slice(head * DH, head * DH + DH)
        theirs = slice(2 * half + head * DH, 2 * half + head * DH + DH)
        value_columns = slice(half + head * DH, half + head * DH + DH)
        query = jnp.concatenate(
            [
                jnp.where(encoder_side, across[:, columns], part[:, theirs])
                for across, part in zip(queries[::2], queries[1::2])
            ],
            axis=0,
        )
        scores = jnp.concatenate(
            [
                lax.dot_general(
                    query, piece[:, columns], (((1,), (1,)), ((), ())), preferred_element_type=F32
                )
                for piece in pieces
            ],
            axis=1,
        )
        scores = jnp.where(valid, scores * DH ** (-0.5), -1e30)
        best = jnp.max(scores, axis=1, keepdims=True)
        weights = jnp.exp(scores - best).astype(BF16)
        total = jnp.sum(weights.astype(F32), axis=1, keepdims=True)
        accum = jnp.zeros((query.shape[0], DH), F32)
        for index, piece in enumerate(pieces):
            accum += jnp.dot(
                weights[:, index * rows : (index + 1) * rows],
                piece[:, value_columns],
                preferred_element_type=F32,
            )
        attended = (accum / total).astype(BF16)
        for chunk, out in enumerate(outs):
            out[:, columns] = attended[chunk * per_chunk : (chunk + 1) * per_chunk]


def attention(segment, queries, pieces, lengths):
    rows, columns = queries[0][0].shape
    chunks = len(queries)
    heads = columns // 2 // DH
    keys = pieces[0].shape[0] * len(pieces)
    vmem = pl.BlockSpec(memory_space=pltpu.VMEM)
    scalars = jnp.concatenate([jnp.asarray(segment, jnp.int32).reshape(1), lengths])
    return pl.pallas_call(
        functools.partial(attention_kernel, heads, pieces[0].shape[0], chunks),
        out_shape=[jax.ShapeDtypeStruct((rows, columns // 2), BF16)] * chunks,
        in_specs=[pl.BlockSpec(memory_space=pltpu.SMEM)] + [vmem] * (2 * chunks + len(pieces)),
        out_specs=[vmem] * chunks,
        compiler_params=pltpu.CompilerParams(vmem_limit_bytes=16 * 1024 * 1024),
        cost_estimate=pl.CostEstimate(
            flops=2 * chunks * rows * keys * columns,
            bytes_accessed=4 * chunks * rows * columns + 2 * keys * columns,
            transcendentals=chunks * rows * heads * keys,
        ),
        name="attention",
    )(scalars, *[array for pair in queries for array in pair], *pieces)


def exchange(part, payload, seq, *after):
    encoder_side = lax.axis_index("segment") == 0
    across = swap(payload, "segment", 1)
    here = jnp.where(encoder_side, part[:, : payload.shape[1]], across)
    if seq == 4:
        there = swap(tie(here, *after) if after else here, "seq", 2)
        return [here, there, swap(here, "seq", 1), swap(there, "seq", 1)], across
    everything = lax.all_gather(here, "seq", axis=0)
    return [everything[place] for place in range(seq)], across


def gather_lengths(lengths, seq):
    if seq == 4:
        chip = jnp.concatenate([lengths, swap(lengths, "seq", 2)])
        return jnp.concatenate([chip, swap(chip, "seq", 1)])
    return lax.all_gather(lengths, "seq", axis=0, tiled=True)


def pick_kernel(scalars, raw, first, second, *refs):
    outs, row_out, buffer, sems = refs[:-3], refs[-3], refs[-2], refs[-1]
    rows = outs[0].shape[0]
    piece = row_out.shape[0]
    start = pl.multiple_of(scalars[1] * piece, piece)
    fetch = pltpu.make_async_copy(raw.at[pl.ds(start, piece)], buffer, sems.at[len(outs)])
    for index, ref in enumerate((first, second)):

        @pl.when(scalars[0] == index)
        def _(ref=ref):
            for chunk, out in enumerate(outs):
                pltpu.make_async_copy(
                    ref.at[pl.ds(chunk * rows, rows)], out, sems.at[chunk]
                ).start()

    fetch.start()
    fetch.wait()
    row_out[...] = jnp.swapaxes(buffer[...], 0, 1)[1]
    for chunk, out in enumerate(outs):
        pltpu.make_async_copy(out, out, sems.at[chunk]).wait()


def pick(which, first, second, weights, block, piece):
    rows, columns = first.shape
    width = weights.shape[2]
    hbm = pl.BlockSpec(memory_space=pltpu.HBM)
    scalars = jnp.stack([jnp.asarray(which, jnp.int32), jnp.asarray(block, jnp.int32)])
    return pl.pallas_call(
        pick_kernel,
        out_shape=[pltpu.VMEM((rows // CHUNKS, columns), BF16)] * CHUNKS
        + [pltpu.VMEM((piece, width), BF16)],
        in_specs=[pl.BlockSpec(memory_space=pltpu.SMEM)] + [hbm] * 3,
        out_specs=[pl.BlockSpec(memory_space=pltpu.VMEM)] * (CHUNKS + 1),
        scratch_shapes=[
            pltpu.VMEM((piece, 2, width), BF16),
            pltpu.SemaphoreType.DMA((CHUNKS + 1,)),
        ],
        compiler_params=pltpu.CompilerParams(vmem_limit_bytes=62_300_000),
        cost_estimate=pl.CostEstimate(flops=0, bytes_accessed=rows * columns, transcendentals=0),
        name="pick",
    )(scalars, weights, first, second)


def relayout_kernel(half_blocks, order, raw, *refs):
    out, second, buffers, staged, sems = refs[-5:]
    columns = raw.shape[2]
    half = columns // 2
    ahead, rows = buffers.shape[:2]
    per = columns // rows
    steps = out.shape[0] // rows

    def copy(step):
        start = pl.multiple_of(order[step // per] * columns + step % per * rows, rows)
        slot = step % ahead
        return pltpu.make_async_copy(
            raw.at[pl.ds(start, rows)], buffers.at[slot], sems.at[slot]
        )

    def store(step):
        return pltpu.make_async_copy(
            staged.at[step % 2], second.at[pl.ds(step * rows, rows)], sems.at[ahead + step % 2]
        )

    def when(step):
        return pl.when(order[step // per] >= half_blocks)

    for step in range(min(ahead - 1, steps)):
        copy(step).start()
    for step in range(steps):
        if step + ahead - 1 < steps:
            copy(step + ahead - 1).start()
        copy(step).wait()
        there = slice(step * rows, (step + 1) * rows)
        apart = jnp.swapaxes(buffers[step % ahead], 0, 1)
        out[there, :half] = apart[0, :, :half]
        out[there, half:columns] = apart[1, :, :half]
        out[there, columns : columns + half] = apart[0, :, half:]
        out[there, columns + half :] = apart[1, :, half:]
        if step > 1:
            when(step - 2)(lambda: store(step - 2).wait())

        @when(step)
        def _(step=step, apart=apart):
            staged[step % 2] = apart[1]
            store(step).start()

    for step in range(max(0, steps - 2), steps):
        when(step)(lambda: store(step).wait())


def relayout(weights, order, *after):
    width, _, columns = weights.shape
    rows = min(columns, 512)
    hbm = pl.BlockSpec(memory_space=pltpu.HBM)
    return pl.pallas_call(
        functools.partial(relayout_kernel, width // columns // 2),
        out_shape=[
            pltpu.VMEM((width, 2 * columns), BF16),
            jax.ShapeDtypeStruct((width, columns), BF16),
        ],
        in_specs=[pl.BlockSpec(memory_space=pltpu.SMEM), hbm]
        + [pl.BlockSpec(memory_space=pl.ANY)] * len(after),
        out_specs=[pl.BlockSpec(memory_space=pltpu.VMEM), hbm],
        scratch_shapes=[
            pltpu.VMEM((4, rows, 2, columns), BF16),
            pltpu.VMEM((2, rows, columns), BF16),
            pltpu.SemaphoreType.DMA((6,)),
        ],
        compiler_params=pltpu.CompilerParams(vmem_limit_bytes=32 * 1024 * 1024),
        cost_estimate=pl.CostEstimate(
            flops=0, bytes_accessed=8 * width * columns, transcendentals=0
        ),
        name="relayout",
    )(order, weights, *after)


def project_kernel(first, count, started, final, which, *refs):
    refs = refs[:-1]
    blocks, weights, refs = refs[:count], refs[count], refs[count + 1 :]
    depth = blocks[0].shape[1]
    half = weights.shape[1] // 2
    tile = min(half, 512)

    def columns(start):
        total = refs[0][:, start : start + tile] if started else None
        for index, block in enumerate(blocks):
            row = (first + index) * depth
            term = jnp.dot(
                block[...],
                weights[row : row + depth, start : start + tile],
                preferred_element_type=F32,
            )
            total = term if total is None else total + term
        return total

    for start in range(0, half, tile):
        there = slice(start, start + tile)
        behind = slice(half + start, half + start + tile)
        lower, upper = columns(start), columns(half + start)
        if final:
            out, payload = refs[-2:]
            lower, upper = lower.astype(BF16), upper.astype(BF16)
            payload[:, there] = jnp.where(which[0] == 0, upper, lower)
        else:
            out = refs[-1]
        out[:, there] = lower
        out[:, behind] = upper


def project(segment, blocks, first, weights, total, final):
    rows, depth = blocks[0].shape
    width = weights.shape[1]
    started = total is not None
    vmem = pl.BlockSpec(memory_space=pltpu.VMEM)
    if final:
        shapes = [
            jax.ShapeDtypeStruct((rows, width), BF16),
            jax.ShapeDtypeStruct((rows, width // 2), BF16),
        ]
    else:
        shapes = [jax.ShapeDtypeStruct((rows, width), F32)]
    *outs, weights = pl.pallas_call(
        functools.partial(project_kernel, first, len(blocks), started, final),
        out_shape=shapes + [pltpu.VMEM(weights.shape, BF16)],
        in_specs=[pl.BlockSpec(memory_space=pltpu.SMEM)] + [vmem] * (len(blocks) + 1 + started),
        out_specs=[vmem] * (len(shapes) + 1),
        input_output_aliases={1 + len(blocks): len(shapes)},
        compiler_params=pltpu.CompilerParams(vmem_limit_bytes=16 * 1024 * 1024),
        cost_estimate=pl.CostEstimate(
            flops=2 * len(blocks) * rows * depth * width,
            bytes_accessed=2 * len(blocks) * depth * width,
            transcendentals=0,
        ),
        name="project",
    )(
        jnp.asarray(segment, jnp.int32).reshape(1),
        *blocks,
        weights,
        *([total] if started else []),
    )
    return weights, *outs


def output_rows_kernel(block, raw, *refs):
    out, buffer, sem = refs[-3:]
    rows = out.shape[0]
    start = pl.multiple_of(block[0] * rows, rows)
    copy = pltpu.make_async_copy(raw.at[pl.ds(start, rows)], buffer, sem)
    copy.start()
    copy.wait()
    out[...] = jnp.swapaxes(buffer[...], 0, 1)[1]


def output_rows(weights, block, rows, *after):
    _, _, columns = weights.shape
    return pl.pallas_call(
        output_rows_kernel,
        out_shape=pltpu.VMEM((rows, columns), BF16),
        in_specs=[
            pl.BlockSpec(memory_space=pltpu.SMEM),
            pl.BlockSpec(memory_space=pltpu.HBM),
        ]
        + [pl.BlockSpec(memory_space=pl.ANY)] * len(after),
        out_specs=pl.BlockSpec(memory_space=pltpu.VMEM),
        scratch_shapes=[pltpu.VMEM((rows, 2, columns), BF16), pltpu.SemaphoreType.DMA],
        compiler_params=pltpu.CompilerParams(vmem_limit_bytes=50 * 1024 * 1024),
        cost_estimate=pl.CostEstimate(
            flops=0, bytes_accessed=rows * columns, transcendentals=0
        ),
        name="output_rows",
    )(jnp.asarray(block, jnp.int32).reshape(1), weights, *after)


def output_kernel(blocks, scalars, mine, other, weights, states, *refs):
    outs = refs[-len(blocks) :]
    encoder_side = scalars[0] == 0
    first = jnp.where(encoder_side, mine[...], other[...])
    second = jnp.where(encoder_side, other[...], mine[...])
    attended = jnp.concatenate([first, second], axis=1)
    for index, out in zip(blocks, outs):
        each = out.shape[1]
        rows = slice(index * each, (index + 1) * each)
        term = lax.dot_general(
            attended, weights[rows, :], (((1,), (1,)), ((), ())), preferred_element_type=F32
        )
        start = pl.multiple_of(scalars[1 + 2 * index], 128)
        residual = states[:, pl.ds(start, each)].astype(F32)
        out[...] = (term + jnp.where(scalars[2 + 2 * index] == 1, residual, 0)).astype(BF16)


def output_blocks(mine, other, weights, states, chunk, scalars, count, blocks, *after):
    rows, half = mine.shape
    each = weights.shape[0] // count
    vmem = pl.BlockSpec(memory_space=pltpu.VMEM)
    here = pl.BlockSpec((rows, states.shape[1]), lambda i: (chunk, 0))
    return pl.pallas_call(
        functools.partial(output_kernel, blocks),
        out_shape=[jax.ShapeDtypeStruct((rows, each), BF16)] * len(blocks),
        grid=(1,),
        in_specs=[pl.BlockSpec(memory_space=pltpu.SMEM)]
        + [vmem] * 3
        + [here]
        + [pl.BlockSpec(memory_space=pl.ANY)] * len(after),
        out_specs=[vmem] * len(blocks),
        compiler_params=pltpu.CompilerParams(vmem_limit_bytes=16 * 1024 * 1024),
        cost_estimate=pl.CostEstimate(
            flops=4 * rows * half * each * len(blocks),
            bytes_accessed=4 * half * each * len(blocks),
            transcendentals=0,
        ),
        name="output_blocks",
    )(scalars, mine, other, weights, states, *after)


def assemble_kernel(each, count, after, scalars, *refs):
    states, sources = refs[after], refs[after + 1 : -3]
    out, held, sems = refs[-3:]
    parts = [out.at[pl.ds(k * each, each)] for k in range(count)]
    fetch = pltpu.make_async_copy(states, held, sems.at[count])
    fetch.start()
    for k in range(count):
        source, row = scalars[2 * k], pl.multiple_of(scalars[1 + 2 * k], each)
        for index, ref in enumerate(sources):

            @pl.when(source == index)
            def _(ref=ref, k=k, row=row):
                pltpu.make_async_copy(ref.at[pl.ds(row, each)], parts[k], sems.at[k]).start()

    for k in range(count):
        pltpu.make_async_copy(parts[k], parts[k], sems.at[k]).wait()
    fetch.wait()


def assemble(sources, scalars, each, count, states, *after):
    columns = sources[0].shape[1]
    vmem = pl.BlockSpec(memory_space=pltpu.VMEM)
    return pl.pallas_call(
        functools.partial(assemble_kernel, each, count, len(after)),
        out_shape=[
            pltpu.VMEM((each * count, columns), BF16),
            pltpu.VMEM(states.shape, BF16),
        ],
        in_specs=[pl.BlockSpec(memory_space=pltpu.SMEM)] * (1 + len(after))
        + [pl.BlockSpec(memory_space=pltpu.HBM)]
        + [pl.BlockSpec(memory_space=pl.ANY)] * len(sources),
        out_specs=[vmem, vmem],
        scratch_shapes=[pltpu.SemaphoreType.DMA((count + 1,))],
        compiler_params=pltpu.CompilerParams(vmem_limit_bytes=48 * 1024 * 1024),
        cost_estimate=pl.CostEstimate(
            flops=0, bytes_accessed=4 * each * count * columns, transcendentals=0
        ),
        name="assemble",
    )(scalars, *after, states, *sources)


def local(enc_states, dec_states, section_weights, group_lengths):
    segment = lax.axis_index("segment")
    encoder_side = segment == 0
    place = lax.axis_index("mp")
    size = lax.axis_size("mp")
    seq = lax.axis_size("seq")
    raw = section_weights[0]
    width, _, columns = raw.shape
    each = width // (2 * size)

    order = jnp.stack([jnp.asarray(block, jnp.int32) for block in line_order(size, place)])
    parts = 4 if seq == 4 else 1
    me = lax.axis_index("seq")
    lengths = gather_lengths(group_lengths, seq)
    pieces_ahead = 2
    ahead_rows = width // (2 * parts * pieces_ahead)
    first = me * pieces_ahead if parts == 4 else 0
    *states, ahead = pick(segment, enc_states, dec_states, raw, first, ahead_rows)
    rows = states[0].shape[0]
    ahead = [ahead, output_rows(raw, first + 1, ahead_rows, ahead, lengths)]
    along = []
    if size == 4:
        beside = [swap(part, "mp", 1) for part in states]
        across = [swap(states[0], "mp", 2)]
        last = [swap(across[0], "mp", 1)]
        for part in states[1:]:
            part = tie(part, across[-1], beside[0], *ahead)
            across.append(swap(part, "mp", 2))
            last.append(swap(across[-1], "mp", 1))
        blocks = [states, beside, across]
    else:
        blocks = line_gather(jnp.concatenate(states, axis=0), "mp")
        blocks = [
            [block[chunk * rows : (chunk + 1) * rows] for chunk in range(CHUNKS)]
            for block in blocks
        ]
        across, last = blocks[1], blocks.pop()
    ahead = [lax.ppermute(part, "segment", [(1, 0)]) for part in ahead]
    weights, output = relayout(raw, order, across[0])
    if parts == 4:
        along = [
            swap(tie(part, *after), "seq", 2)
            for part, after in zip(ahead, ((across[0],), (across[-1], output)))
        ]

    pieces = [[] for _ in range(seq)]
    query_parts = []
    for chunk in range(CHUNKS):
        terms = [block[chunk] for block in blocks]
        if chunk:
            weights, total = project(segment, terms, 0, weights, None, False)
            weights, part, payload = project(
                segment, [last[chunk]], size - 1, weights, total, True
            )
            payload = tie(payload, got)
        else:
            terms[0] = tie(terms[0], *along[:1])
            weights, part, payload = project(
                segment, terms + [last[chunk]], 0, weights, None, True
            )
        memory, got = exchange(part, payload, seq, *along[1:])
        for source, piece in enumerate(memory):
            pieces[source].append(piece)
        query_parts.append((got, part))
    flat = [piece for source in pieces for piece in source]

    low = ahead + along
    if parts == 4:
        low = [tie(part, pieces[1][0]) for part in low]
        low += [swap(part, "seq", 1) for part in low]
    targets = [place ^ k if size == 4 else jnp.int32(k) for k in range(size)]
    inverse = None if size == 4 else jnp.argsort(order)
    grain = math.gcd(each, ahead_rows)
    sources, residual = [], [segment]
    for target in targets:
        for offset in range(0, each, grain):
            start = target * each + offset
            block = (width // 2 + start) // columns
            block = block ^ place if inverse is None else inverse[block]
            row = block * columns + lax.rem(start, columns)
            part = 0
            per = width // (2 * parts)
            if parts == 4:
                part = (start // per) ^ me
                part = ((part & 1) << 1) | (part >> 1)
            part = part * pieces_ahead + lax.rem(start, per) // ahead_rows
            low_row = lax.rem(start, ahead_rows)
            sources.append(jnp.where(encoder_side, part, len(low)))
            sources.append(jnp.where(encoder_side, low_row, row))
        start = segment * (width // 2) + target * each - place * columns
        inside = (start >= 0) & (start < columns)
        residual += [jnp.where(inside, start, 0), inside]
    sources = jnp.stack([jnp.asarray(value, jnp.int32) for value in sources])
    residual = jnp.stack([jnp.asarray(value, jnp.int32) for value in residual])
    final, held_states = assemble(
        low + [output], sources, grain, width // (2 * grain), dec_states
    )

    pairs, far, far_got, near = [], [], [], []
    for part in attention(segment, query_parts, flat, lengths):
        pairs.append((part, swap(part, "segment", 1)))
    for chunk, pair in enumerate(pairs):
        far += output_blocks(*pair, final, held_states, chunk, residual, size, (size - 1,))
        got = far[-1]
        if size == 4:
            got = swap(tie(got, far_got[-1]) if far_got else got, "mp", 1)
        far_got.append(got)
    for chunk, pair in enumerate(pairs):
        after = far_got[0] if chunk else far[-1]
        blocks = tuple(range(size - 1))
        near.append(
            output_blocks(*pair, final, held_states, chunk, residual, size, blocks, after)
        )
    outputs = line_scatter(near, far_got, "mp")
    return jnp.concatenate(outputs, axis=0).astype(BF16)


def solution(mesh):
    in_specs = (P("seq", "mp"), P("seq", "mp"), P("segment", None, None, "mp"), P("seq"))
    out_specs = P("seq", ("segment", "mp"))
    return jax.shard_map(local, mesh=mesh, in_specs=in_specs, out_specs=out_specs, check_vma=False)
```

```python
import functools
import math

import jax
import jax.numpy as jnp
from jax import lax
from jax.experimental import pallas as pl
from jax.experimental.pallas import tpu as pltpu
from jax.sharding import PartitionSpec as P

DH = 256
GROUP = 128
CHUNKS = 2
BF16 = jnp.bfloat16
F32 = jnp.float32


def tie(value, *after):
    return lax.optimization_barrier((value, *after))[0]


def swap(value, axis, distance):
    return lax.ppermute(value, axis, [(i, i ^ distance) for i in range(lax.axis_size(axis))])


def line_order(size, me):
    if size == 4:
        return [me, me ^ 1, me ^ 2, me ^ 3]
    order = [me]
    for step in range(1, size // 2 + 1):
        order.append(lax.rem(me - step + size, size))
        if len(order) < size:
            order.append(lax.rem(me + step, size))
    return order


def line_gather(own, axis):
    size = lax.axis_size(axis)
    blocks = [own]
    up = down = own
    for step in range(1, size // 2 + 1):
        up = lax.ppermute(up, axis, [(i, (i + 1) % size) for i in range(size)])
        blocks.append(up)
        if len(blocks) < size:
            down = lax.ppermute(down, axis, [(i, (i - 1) % size) for i in range(size)])
            blocks.append(down)
    return blocks


def line_scatter(near, far, axis):
    if lax.axis_size(axis) == 4:
        across = [
            swap((blocks[2].astype(F32) + got.astype(F32)).astype(BF16), axis, 2)
            for blocks, got in zip(near, far)
        ]
        beside = [swap(tie(blocks[1], *far), axis, 1) for blocks in near]
        return [
            blocks[0].astype(F32) + one.astype(F32) + two.astype(F32)
            for blocks, one, two in zip(near, beside, across)
        ]
    return [
        lax.psum_scatter(
            jnp.concatenate([*blocks, last], axis=1), axis, scatter_dimension=1, tiled=True
        ).astype(F32)
        for blocks, last in zip(near, far)
    ]


def attention_kernel(heads, rows, chunks, scalars, *refs):
    queries, pieces, outs = refs[: 2 * chunks], refs[2 * chunks : -chunks], refs[-chunks:]
    encoder_side = scalars[0] == 0
    half = heads * DH
    per_piece = rows // GROUP
    per_chunk = outs[0].shape[0]
    masks = []
    for index in range(len(pieces)):
        for group in range(per_piece):
            column = lax.broadcasted_iota(jnp.int32, (1, GROUP), 1)
            masks.append(column < scalars[1 + index * per_piece + group])
    valid = jnp.concatenate(masks, axis=1)
    for head in range(heads):
        columns = slice(head * DH, head * DH + DH)
        theirs = slice(2 * half + head * DH, 2 * half + head * DH + DH)
        value_columns = slice(half + head * DH, half + head * DH + DH)
        query = jnp.concatenate(
            [
                jnp.where(encoder_side, across[:, columns], part[:, theirs])
                for across, part in zip(queries[::2], queries[1::2])
            ],
            axis=0,
        )
        scores = jnp.concatenate(
            [
                lax.dot_general(
                    query, piece[:, columns], (((1,), (1,)), ((), ())), preferred_element_type=F32
                )
                for piece in pieces
            ],
            axis=1,
        )
        scores = jnp.where(valid, scores * DH ** (-0.5), -1e30)
        best = jnp.max(scores, axis=1, keepdims=True)
        weights = jnp.exp(scores - best).astype(BF16)
        total = jnp.sum(weights.astype(F32), axis=1, keepdims=True)
        accum = jnp.zeros((query.shape[0], DH), F32)
        for index, piece in enumerate(pieces):
            accum += jnp.dot(
                weights[:, index * rows : (index + 1) * rows],
                piece[:, value_columns],
                preferred_element_type=F32,
            )
        attended = (accum * (1.0 / total)).astype(BF16)
        for chunk, out in enumerate(outs):
            out[:, columns] = attended[chunk * per_chunk : (chunk + 1) * per_chunk]


def attention(segment, queries, pieces, lengths):
    rows, columns = queries[0][0].shape
    chunks = len(queries)
    heads = columns // 2 // DH
    keys = pieces[0].shape[0] * len(pieces)
    vmem = pl.BlockSpec(memory_space=pltpu.VMEM)
    scalars = jnp.concatenate([jnp.asarray(segment, jnp.int32).reshape(1), lengths])
    return pl.pallas_call(
        functools.partial(attention_kernel, heads, pieces[0].shape[0], chunks),
        out_shape=[jax.ShapeDtypeStruct((rows, columns // 2), BF16)] * chunks,
        in_specs=[pl.BlockSpec(memory_space=pltpu.SMEM)] + [vmem] * (2 * chunks + len(pieces)),
        out_specs=[vmem] * chunks,
        compiler_params=pltpu.CompilerParams(vmem_limit_bytes=16 * 1024 * 1024),
        cost_estimate=pl.CostEstimate(
            flops=2 * chunks * rows * keys * columns,
            bytes_accessed=4 * chunks * rows * columns + 2 * keys * columns,
            transcendentals=chunks * rows * heads * keys,
        ),
        name="attention",
    )(scalars, *[array for pair in queries for array in pair], *pieces)


def exchange(part, payload, seq, *after):
    encoder_side = lax.axis_index("segment") == 0
    across = swap(payload, "segment", 1)
    here = jnp.where(encoder_side, part[:, : payload.shape[1]], across)
    if seq == 4:
        there = swap(tie(here, *after) if after else here, "seq", 2)
        return [here, there, swap(here, "seq", 1), swap(there, "seq", 1)], across
    everything = lax.all_gather(here, "seq", axis=0)
    return [everything[place] for place in range(seq)], across


def gather_lengths(lengths, seq):
    if seq == 4:
        chip = jnp.concatenate([lengths, swap(lengths, "seq", 2)])
        return jnp.concatenate([chip, swap(chip, "seq", 1)])
    return lax.all_gather(lengths, "seq", axis=0, tiled=True)


def pick_kernel(scalars, raw, first, second, *refs):
    outs, row_out, buffer, sems = refs[:-3], refs[-3], refs[-2], refs[-1]
    rows = outs[0].shape[0]
    piece = row_out.shape[0]
    start = pl.multiple_of(scalars[1] * piece, piece)
    half = piece // 2
    parts = [slice(0, half), slice(half, piece)]
    fetches = [
        pltpu.make_async_copy(
            raw.at[pl.ds(start + index * half, half)],
            buffer.at[pl.ds(index * half, half)],
            sems.at[len(outs) + index],
        )
        for index in range(2)
    ]
    for fetch in fetches:
        fetch.start()
    for index, ref in enumerate((first, second)):

        @pl.when(scalars[0] == index)
        def _(ref=ref):
            for chunk, out in enumerate(outs):
                pltpu.make_async_copy(
                    ref.at[pl.ds(chunk * rows, rows)], out, sems.at[chunk]
                ).start()

    for fetch, part in zip(fetches, parts):
        fetch.wait()
        row_out[part] = jnp.swapaxes(buffer[part], 0, 1)[1]
    for chunk, out in enumerate(outs):
        pltpu.make_async_copy(out, out, sems.at[chunk]).wait()


def pick(which, first, second, weights, block, piece):
    rows, columns = first.shape
    width = weights.shape[2]
    hbm = pl.BlockSpec(memory_space=pltpu.HBM)
    scalars = jnp.stack([jnp.asarray(which, jnp.int32), jnp.asarray(block, jnp.int32)])
    return pl.pallas_call(
        pick_kernel,
        out_shape=[pltpu.VMEM((rows // CHUNKS, columns), BF16)] * CHUNKS
        + [pltpu.VMEM((piece, width), BF16)],
        in_specs=[pl.BlockSpec(memory_space=pltpu.SMEM)] + [hbm] * 3,
        out_specs=[pl.BlockSpec(memory_space=pltpu.VMEM)] * (CHUNKS + 1),
        scratch_shapes=[
            pltpu.VMEM((piece, 2, width), BF16),
            pltpu.SemaphoreType.DMA((CHUNKS + 2,)),
        ],
        compiler_params=pltpu.CompilerParams(vmem_limit_bytes=62_300_000),
        cost_estimate=pl.CostEstimate(flops=0, bytes_accessed=rows * columns, transcendentals=0),
        name="pick",
    )(scalars, weights, first, second)


def relayout_kernel(half_blocks, order, raw, *refs):
    out, second, buffers, staged, sems = refs[-5:]
    columns = raw.shape[2]
    half = columns // 2
    ahead, rows = buffers.shape[:2]
    per = columns // rows
    steps = out.shape[0] // rows

    def copy(step):
        start = pl.multiple_of(order[step // per] * columns + step % per * rows, rows)
        slot = step % ahead
        return pltpu.make_async_copy(
            raw.at[pl.ds(start, rows)], buffers.at[slot], sems.at[slot]
        )

    def store(step):
        return pltpu.make_async_copy(
            staged.at[step % 2], second.at[pl.ds(step * rows, rows)], sems.at[ahead + step % 2]
        )

    def when(step):
        return pl.when(order[step // per] >= half_blocks)

    for step in range(min(ahead - 1, steps)):
        copy(step).start()
    for step in range(steps):
        if step + ahead - 1 < steps:
            copy(step + ahead - 1).start()
        copy(step).wait()
        there = slice(step * rows, (step + 1) * rows)
        apart = jnp.swapaxes(buffers[step % ahead], 0, 1)
        out[there, :half] = apart[0, :, :half]
        out[there, half:columns] = apart[1, :, :half]
        out[there, columns : columns + half] = apart[0, :, half:]
        out[there, columns + half :] = apart[1, :, half:]
        if step > 1:
            when(step - 2)(lambda: store(step - 2).wait())

        @when(step)
        def _(step=step, apart=apart):
            staged[step % 2] = apart[1]
            store(step).start()

    for step in range(max(0, steps - 2), steps):
        when(step)(lambda: store(step).wait())


def relayout(weights, order, *after):
    width, _, columns = weights.shape
    rows = min(columns, 512)
    hbm = pl.BlockSpec(memory_space=pltpu.HBM)
    return pl.pallas_call(
        functools.partial(relayout_kernel, width // columns // 2),
        out_shape=[
            pltpu.VMEM((width, 2 * columns), BF16),
            jax.ShapeDtypeStruct((width, columns), BF16),
        ],
        in_specs=[pl.BlockSpec(memory_space=pltpu.SMEM), hbm]
        + [pl.BlockSpec(memory_space=pl.ANY)] * len(after),
        out_specs=[pl.BlockSpec(memory_space=pltpu.VMEM), hbm],
        scratch_shapes=[
            pltpu.VMEM((4, rows, 2, columns), BF16),
            pltpu.VMEM((2, rows, columns), BF16),
            pltpu.SemaphoreType.DMA((6,)),
        ],
        compiler_params=pltpu.CompilerParams(vmem_limit_bytes=32 * 1024 * 1024),
        cost_estimate=pl.CostEstimate(
            flops=0, bytes_accessed=8 * width * columns, transcendentals=0
        ),
        name="relayout",
    )(order, weights, *after)


def project_kernel(first, count, started, final, which, *refs):
    refs = refs[:-1]
    blocks, weights, refs = refs[:count], refs[count], refs[count + 1 :]
    depth = blocks[0].shape[1]
    half = weights.shape[1] // 2
    tile = min(half, 512)

    def columns(start):
        total = refs[0][:, start : start + tile] if started else None
        for index, block in enumerate(blocks):
            row = (first + index) * depth
            term = jnp.dot(
                block[...],
                weights[row : row + depth, start : start + tile],
                preferred_element_type=F32,
            )
            total = term if total is None else total + term
        return total

    for start in range(0, half, tile):
        there = slice(start, start + tile)
        behind = slice(half + start, half + start + tile)
        lower, upper = columns(start), columns(half + start)
        if final:
            out, payload = refs[-2:]
            lower, upper = lower.astype(BF16), upper.astype(BF16)
            payload[:, there] = jnp.where(which[0] == 0, upper, lower)
        else:
            out = refs[-1]
        out[:, there] = lower
        out[:, behind] = upper


def project(segment, blocks, first, weights, total, final):
    rows, depth = blocks[0].shape
    width = weights.shape[1]
    started = total is not None
    vmem = pl.BlockSpec(memory_space=pltpu.VMEM)
    if final:
        shapes = [
            jax.ShapeDtypeStruct((rows, width), BF16),
            jax.ShapeDtypeStruct((rows, width // 2), BF16),
        ]
    else:
        shapes = [jax.ShapeDtypeStruct((rows, width), F32)]
    *outs, weights = pl.pallas_call(
        functools.partial(project_kernel, first, len(blocks), started, final),
        out_shape=shapes + [pltpu.VMEM(weights.shape, BF16)],
        in_specs=[pl.BlockSpec(memory_space=pltpu.SMEM)] + [vmem] * (len(blocks) + 1 + started),
        out_specs=[vmem] * (len(shapes) + 1),
        input_output_aliases={1 + len(blocks): len(shapes)},
        compiler_params=pltpu.CompilerParams(vmem_limit_bytes=16 * 1024 * 1024),
        cost_estimate=pl.CostEstimate(
            flops=2 * len(blocks) * rows * depth * width,
            bytes_accessed=2 * len(blocks) * depth * width,
            transcendentals=0,
        ),
        name="project",
    )(
        jnp.asarray(segment, jnp.int32).reshape(1),
        *blocks,
        weights,
        *([total] if started else []),
    )
    return weights, *outs


def output_rows_kernel(block, raw, *refs):
    out, buffer, sem = refs[-3:]
    rows = out.shape[0]
    start = pl.multiple_of(block[0] * rows, rows)
    copy = pltpu.make_async_copy(raw.at[pl.ds(start, rows)], buffer, sem)
    copy.start()
    copy.wait()
    out[...] = jnp.swapaxes(buffer[...], 0, 1)[1]


def output_rows(weights, block, rows, *after):
    _, _, columns = weights.shape
    return pl.pallas_call(
        output_rows_kernel,
        out_shape=pltpu.VMEM((rows, columns), BF16),
        in_specs=[
            pl.BlockSpec(memory_space=pltpu.SMEM),
            pl.BlockSpec(memory_space=pltpu.HBM),
        ]
        + [pl.BlockSpec(memory_space=pl.ANY)] * len(after),
        out_specs=pl.BlockSpec(memory_space=pltpu.VMEM),
        scratch_shapes=[pltpu.VMEM((rows, 2, columns), BF16), pltpu.SemaphoreType.DMA],
        compiler_params=pltpu.CompilerParams(vmem_limit_bytes=50 * 1024 * 1024),
        cost_estimate=pl.CostEstimate(
            flops=0, bytes_accessed=rows * columns, transcendentals=0
        ),
        name="output_rows",
    )(jnp.asarray(block, jnp.int32).reshape(1), weights, *after)


def output_kernel(blocks, scalars, mine, other, weights, states, *refs):
    outs = refs[-len(blocks) :]
    encoder_side = scalars[0] == 0
    first = jnp.where(encoder_side, mine[...], other[...])
    second = jnp.where(encoder_side, other[...], mine[...])
    attended = jnp.concatenate([first, second], axis=1)
    for index, out in zip(blocks, outs):
        each = out.shape[1]
        rows = slice(index * each, (index + 1) * each)
        term = lax.dot_general(
            attended, weights[rows, :], (((1,), (1,)), ((), ())), preferred_element_type=F32
        )
        start = pl.multiple_of(scalars[1 + 2 * index], 128)
        residual = states[:, pl.ds(start, each)].astype(F32)
        out[...] = (term + jnp.where(scalars[2 + 2 * index] == 1, residual, 0)).astype(BF16)


def output_blocks(mine, other, weights, states, chunk, scalars, count, blocks, *after):
    rows, half = mine.shape
    each = weights.shape[0] // count
    vmem = pl.BlockSpec(memory_space=pltpu.VMEM)
    here = pl.BlockSpec((rows, states.shape[1]), lambda i: (chunk, 0))
    return pl.pallas_call(
        functools.partial(output_kernel, blocks),
        out_shape=[jax.ShapeDtypeStruct((rows, each), BF16)] * len(blocks),
        grid=(1,),
        in_specs=[pl.BlockSpec(memory_space=pltpu.SMEM)]
        + [vmem] * 3
        + [here]
        + [pl.BlockSpec(memory_space=pl.ANY)] * len(after),
        out_specs=[vmem] * len(blocks),
        compiler_params=pltpu.CompilerParams(vmem_limit_bytes=16 * 1024 * 1024),
        cost_estimate=pl.CostEstimate(
            flops=4 * rows * half * each * len(blocks),
            bytes_accessed=4 * half * each * len(blocks),
            transcendentals=0,
        ),
        name="output_blocks",
    )(scalars, mine, other, weights, states, *after)


def assemble_kernel(each, count, after, scalars, *refs):
    states, sources = refs[after], refs[after + 1 : -3]
    out, held, sems = refs[-3:]
    parts = [out.at[pl.ds(k * each, each)] for k in range(count)]
    fetch = pltpu.make_async_copy(states, held, sems.at[count])
    fetch.start()
    for k in range(count):
        source, row = scalars[2 * k], pl.multiple_of(scalars[1 + 2 * k], each)
        for index, ref in enumerate(sources):

            @pl.when(source == index)
            def _(ref=ref, k=k, row=row):
                pltpu.make_async_copy(ref.at[pl.ds(row, each)], parts[k], sems.at[k]).start()

    for k in range(count):
        pltpu.make_async_copy(parts[k], parts[k], sems.at[k]).wait()
    fetch.wait()


def assemble(sources, scalars, each, count, states, *after):
    columns = sources[0].shape[1]
    vmem = pl.BlockSpec(memory_space=pltpu.VMEM)
    return pl.pallas_call(
        functools.partial(assemble_kernel, each, count, len(after)),
        out_shape=[
            pltpu.VMEM((each * count, columns), BF16),
            pltpu.VMEM(states.shape, BF16),
        ],
        in_specs=[pl.BlockSpec(memory_space=pltpu.SMEM)] * (1 + len(after))
        + [pl.BlockSpec(memory_space=pltpu.HBM)]
        + [pl.BlockSpec(memory_space=pl.ANY)] * len(sources),
        out_specs=[vmem, vmem],
        scratch_shapes=[pltpu.SemaphoreType.DMA((count + 1,))],
        compiler_params=pltpu.CompilerParams(vmem_limit_bytes=48 * 1024 * 1024),
        cost_estimate=pl.CostEstimate(
            flops=0, bytes_accessed=4 * each * count * columns, transcendentals=0
        ),
        name="assemble",
    )(scalars, *after, states, *sources)


def local(enc_states, dec_states, section_weights, group_lengths):
    segment = lax.axis_index("segment")
    encoder_side = segment == 0
    place = lax.axis_index("mp")
    size = lax.axis_size("mp")
    seq = lax.axis_size("seq")
    raw = section_weights[0]
    width, _, columns = raw.shape
    each = width // (2 * size)

    order = jnp.stack([jnp.asarray(block, jnp.int32) for block in line_order(size, place)])
    parts = 4 if seq == 4 else 1
    me = lax.axis_index("seq")
    lengths = gather_lengths(group_lengths, seq)
    pieces_ahead = 2
    ahead_rows = width // (2 * parts * pieces_ahead)
    first = me * pieces_ahead if parts == 4 else 0
    *states, ahead = pick(segment, enc_states, dec_states, raw, first, ahead_rows)
    rows = states[0].shape[0]
    ahead = [ahead, output_rows(raw, first + 1, ahead_rows, ahead, lengths)]
    along = []
    if size == 4:
        beside = [swap(part, "mp", 1) for part in states]
        across = [swap(states[0], "mp", 2)]
        last = [swap(across[0], "mp", 1)]
        for part in states[1:]:
            part = tie(part, across[-1], beside[0], *ahead)
            across.append(swap(part, "mp", 2))
            last.append(swap(across[-1], "mp", 1))
        blocks = [states, beside, across]
    else:
        blocks = line_gather(jnp.concatenate(states, axis=0), "mp")
        blocks = [
            [block[chunk * rows : (chunk + 1) * rows] for chunk in range(CHUNKS)]
            for block in blocks
        ]
        across, last = blocks[1], blocks.pop()
    ahead = [lax.ppermute(part, "segment", [(1, 0)]) for part in ahead]
    weights, output = relayout(raw, order, across[0])
    if parts == 4:
        along = [
            swap(tie(part, *after), "seq", 2)
            for part, after in zip(ahead, ((across[0],), (across[-1], output)))
        ]

    pieces = [[] for _ in range(seq)]
    query_parts = []
    for chunk in range(CHUNKS):
        terms = [block[chunk] for block in blocks]
        if chunk:
            weights, total = project(segment, terms, 0, weights, None, False)
            weights, part, payload = project(
                segment, [last[chunk]], size - 1, weights, total, True
            )
            payload = tie(payload, got)
        else:
            terms[0] = tie(terms[0], *along[:1])
            weights, part, payload = project(
                segment, terms + [last[chunk]], 0, weights, None, True
            )
        memory, got = exchange(part, payload, seq, *along[1:])
        for source, piece in enumerate(memory):
            pieces[source].append(piece)
        query_parts.append((got, part))
    flat = [piece for source in pieces for piece in source]

    low = ahead + along
    if parts == 4:
        low = [tie(part, pieces[1][0]) for part in low]
        low += [swap(part, "seq", 1) for part in low]
    targets = [place ^ k if size == 4 else jnp.int32(k) for k in range(size)]
    inverse = None if size == 4 else jnp.argsort(order)
    grain = math.gcd(each, ahead_rows)
    sources, residual = [], [segment]
    for target in targets:
        for offset in range(0, each, grain):
            start = target * each + offset
            block = (width // 2 + start) // columns
            block = block ^ place if inverse is None else inverse[block]
            row = block * columns + lax.rem(start, columns)
            part = 0
            per = width // (2 * parts)
            if parts == 4:
                part = (start // per) ^ me
                part = ((part & 1) << 1) | (part >> 1)
            part = part * pieces_ahead + lax.rem(start, per) // ahead_rows
            low_row = lax.rem(start, ahead_rows)
            sources.append(jnp.where(encoder_side, part, len(low)))
            sources.append(jnp.where(encoder_side, low_row, row))
        start = segment * (width // 2) + target * each - place * columns
        inside = (start >= 0) & (start < columns)
        residual += [jnp.where(inside, start, 0), inside]
    sources = jnp.stack([jnp.asarray(value, jnp.int32) for value in sources])
    residual = jnp.stack([jnp.asarray(value, jnp.int32) for value in residual])
    final, held_states = assemble(
        low + [output], sources, grain, width // (2 * grain), dec_states
    )

    pairs, far, far_got, near = [], [], [], []
    for part in attention(segment, query_parts, flat, lengths):
        pairs.append((part, swap(part, "segment", 1)))
    for chunk, pair in enumerate(pairs):
        far += output_blocks(*pair, final, held_states, chunk, residual, size, (size - 1,))
        got = far[-1]
        if size == 4:
            got = swap(tie(got, far_got[-1]) if far_got else got, "mp", 1)
        far_got.append(got)
    for chunk, pair in enumerate(pairs):
        after = far_got[0] if chunk else far[-1]
        blocks = tuple(range(size - 1))
        near.append(
            output_blocks(*pair, final, held_states, chunk, residual, size, blocks, after)
        )
    outputs = line_scatter(near, far_got, "mp")
    return jnp.concatenate(outputs, axis=0).astype(BF16)


def solution(mesh):
    in_specs = (P("seq", "mp"), P("seq", "mp"), P("segment", None, None, "mp"), P("seq"))
    out_specs = P("seq", ("segment", "mp"))
    return jax.shard_map(local, mesh=mesh, in_specs=in_specs, out_specs=out_specs, check_vma=False)
```
